32 devices in a mesh: groups: 2 (over x), gx: 16 (over z, y, core).
Axes of the slice: x: 2, y: 2, z: 4, core: 2. Of those that a mesh axis runs over, the one named last changes fastest.
Arguments:
- activations: bfloat16 [256, 16384], P('groups', 'gx'), parts along dimension 0, may hold values from -400 to 400
- norm_gain: bfloat16 [16384], P('gx'), may hold values from 0.099609375 to 1.8984375
- w_qkv: bfloat16 [16384, 9216], P('gx'), may hold values from -0.046875 to 0.046875
- w_out: bfloat16 [8192, 16384], P(None, 'gx'), may hold values from -0.0625 to 0.0625
- cache_keys: bfloat16 [256, 256, 4, 128], P(('groups', 'gx')), parts along dimension 0, may hold values from -420 to 420
- value_cache_rows: bfloat16 [256, 256, 4, 128], P(('groups', 'gx')), parts along dimension 0, may hold values from -6 to 6
Outputs:
- attention_out: bfloat16 [256, 16384], P('groups', 'gx'), parts along dimension 0
The draws below stay inside these ranges and needn't reach their ends.
There are 2 independent parts, one for each index of `groups`. The reference program is written for one: setup_inputs(seed, part) draws one part's arguments, and reference() takes and returns one part's arrays. A program takes and returns all parts, laid end to end along the dimension named above; an argument that names none is the same for every part. Nothing has to cross between parts.
All inputs are finite; a program needn't handle non-finite values.
Results may differ from the reference program's by a relative error of at most 0.012.
Values may be sent and summed in bfloat16 or wider, within the bound.
No kernel may reach another device: no remote copies, remote signals or barrier semaphores. Data moves between devices by JAX's collectives and lax.ppermute only.
A program may use at most 128 MiB of HBM per device.

```python
import jax
import jax.numpy as jnp
from jax import lax

D = 16384
QUERY_HEADS = 64
KEY_VALUE_HEADS = 4
HEAD_SIZE = 128
CONTEXT_LENGTH = 256
DECODED_ROWS = 128
QUERY_FEATURES = 8192
QKVW = 9216


def draw_activations(key, part):
    key = jax.random.fold_in(key, 11)
    random_base_key, row_key, column_key = jax.random.split(key, 3)
    rotary_base = jnp.clip(jax.random.normal(random_base_key, (DECODED_ROWS, D), jnp.float32), -4.0, 4.0)
    row_scale = 10.0 ** jax.random.uniform(row_key, (DECODED_ROWS, 1), jnp.float32, 0.0, 1.0)
    column_rise = jnp.arange(D, dtype=jnp.float32) / D
    column_scale = 10.0 ** (0.5 * column_rise[None, :] + 0.5 * jax.random.uniform(column_key, (1, D), jnp.float32))
    return (rotary_base * row_scale * column_scale).astype(jnp.bfloat16)


def draw_cache_keys(key, part):
    key = jax.random.fold_in(key, 23)
    random_base_key = jax.random.fold_in(key, 0)
    rotary_base = jnp.clip(jax.random.normal(random_base_key, (DECODED_ROWS, CONTEXT_LENGTH, KEY_VALUE_HEADS, HEAD_SIZE), jnp.float32), -4.0, 4.0)
    return rotary_base.astype(jnp.bfloat16)


def shard_levels(key, dims, pieces, least, largest):
    def one(axis_at, shards_of):
        steps = jax.random.uniform(jax.random.fold_in(jax.random.fold_in(key, 6), axis_at), (shards_of,), jnp.float32, least / len(pieces), largest / len(pieces))
        return jnp.repeat(jnp.exp(steps), dims[axis_at] // shards_of).reshape((-1,) + (1,) * (len(dims) - axis_at - 1))

    loudness = one(*pieces[0])
    for cut in pieces[1:]:
        loudness = loudness * one(*cut)
    return loudness


def scatter_about(rng, extent, deviation, most, cuts=(), kind=jnp.bfloat16):
    values = jax.random.normal(rng, extent, jnp.float32) * deviation
    if len(cuts) > 0:
        values = shard_levels(rng, extent, cuts, -0.22, 0.18) * values
    return jnp.clip(values, min=-most, max=most).astype(kind)


def setup_inputs(seed: int = 0, part: int = 0) -> dict:
    arg_keys = jax.random.split(jax.random.key(seed), 7)
    own_keys = jax.random.split(jax.random.fold_in(arg_keys[6], part), 7)
    activations = draw_activations(jax.random.fold_in(jax.random.fold_in(arg_keys[6], part), 71), part)
    norm_gain = jnp.clip(1.0 + 0.18 * jax.random.normal(arg_keys[1], (D,), jnp.float32), 0.099609375, 1.8984375).astype(jnp.bfloat16)
    w_qkv = scatter_about(arg_keys[2], (D, QKVW), D ** -0.5, 0.046875, ((0, 16),))
    w_out = scatter_about(arg_keys[3], (QUERY_FEATURES, D), QUERY_FEATURES ** -0.5, 0.0625, ((1, 16),))
    cache_keys = draw_cache_keys(jax.random.fold_in(jax.random.fold_in(arg_keys[6], part), 71), part)
    value_cache_rows = scatter_about(own_keys[5], (DECODED_ROWS, CONTEXT_LENGTH, KEY_VALUE_HEADS, HEAD_SIZE), 1.0, 6.0, ((0, 16),))
    return dict(activations=activations, norm_gain=norm_gain, w_qkv=w_qkv, w_out=w_out, cache_keys=cache_keys, value_cache_rows=value_cache_rows)


def apply_rotary(tensor):
    half_dim = HEAD_SIZE // 2
    frequency = jnp.float32(500000.0) ** (-jnp.arange(half_dim, dtype=jnp.float32) * 2.0 / HEAD_SIZE)
    angles = jnp.float32(CONTEXT_LENGTH) * frequency
    cosine = jnp.cos(angles)
    sine_part = jnp.sin(angles)
    first_half = tensor[..., :half_dim]
    second_half = tensor[..., half_dim:]
    return jnp.concatenate([first_half * cosine - second_half * sine_part, second_half * cosine + first_half * sine_part], axis=-1)

def attend(query_rows, fresh_keys, fresh_values, cache_keys, value_cache_rows):
    count_of_rows = query_rows.shape[0]
    grouped_queries = query_rows.reshape(count_of_rows, KEY_VALUE_HEADS, QUERY_HEADS // KEY_VALUE_HEADS, HEAD_SIZE).astype(jnp.float32)
    scaling = 1.0 / jnp.sqrt(jnp.float32(HEAD_SIZE))
    cached_scores = jnp.einsum('rkgd,rtkd->rkgt', grouped_queries, cache_keys.astype(jnp.float32)) * scaling
    own_scores = jnp.einsum('rkgd,rkd->rkg', grouped_queries, fresh_keys.astype(jnp.float32)) * scaling
    highest = jnp.maximum(lax.optimization_barrier(jnp.max(cached_scores, axis=-1)), own_scores)
    cached_exp = jnp.exp(cached_scores - highest[..., None])
    own_exp = jnp.exp(own_scores - highest)
    denominator = lax.optimization_barrier(jnp.sum(cached_exp, axis=-1)) + own_exp
    cached_weights = (cached_exp / denominator[..., None]).astype(jnp.bfloat16)
    own_weights = (own_exp / denominator).astype(jnp.bfloat16)
    combined = jnp.einsum('rkgt,rtkd->rkgd', cached_weights.astype(jnp.float32), value_cache_rows.astype(jnp.float32))
    combined = combined + own_weights.astype(jnp.float32)[..., None] * fresh_values.astype(jnp.float32)[:, :, None, :]
    return combined.reshape(count_of_rows, QUERY_HEADS * HEAD_SIZE).astype(jnp.bfloat16)

def reference(activations, norm_gain, w_qkv, w_out, cache_keys, value_cache_rows):
    wide_acts = activations.astype(jnp.float32)
    squares = lax.optimization_barrier(jnp.sum(wide_acts * wide_acts, axis=1))
    inverse_rms = lax.rsqrt(squares / D + 1e-05)
    scaled = (wide_acts * norm_gain.astype(jnp.float32)).astype(jnp.bfloat16)
    projected_rows = jnp.dot(scaled, w_qkv, preferred_element_type=jnp.float32) * inverse_rms[:, None]
    query_rows = apply_rotary(projected_rows[:, :QUERY_FEATURES].reshape(DECODED_ROWS, QUERY_HEADS, HEAD_SIZE)).astype(jnp.bfloat16)
    fresh_keys = apply_rotary(projected_rows[:, QUERY_FEATURES:QUERY_FEATURES + KEY_VALUE_HEADS * HEAD_SIZE].reshape(DECODED_ROWS, KEY_VALUE_HEADS, HEAD_SIZE)).astype(jnp.bfloat16)
    fresh_values = projected_rows[:, QUERY_FEATURES + KEY_VALUE_HEADS * HEAD_SIZE:].reshape(DECODED_ROWS, KEY_VALUE_HEADS, HEAD_SIZE).astype(jnp.bfloat16)
    attended = attend(query_rows, fresh_keys, fresh_values, cache_keys, value_cache_rows)
    return jnp.dot(attended, w_out, preferred_element_type=jnp.float32).astype(jnp.bfloat16)
```

```python
import functools

import jax
import jax.numpy as jnp
from jax import lax
from jax.experimental import pallas as pl
from jax.experimental.pallas import tpu as pltpu
from jax.sharding import PartitionSpec as P

D = 16384
QUERY_HEADS = 64
KEY_VALUE_HEADS = 4
HEAD_SIZE = 128
CONTEXT_LENGTH = 256
GROUP = QUERY_HEADS // KEY_VALUE_HEADS
QUERY_WIDTH = QUERY_HEADS * HEAD_SIZE
QKVW = QUERY_WIDTH + 2 * KEY_VALUE_HEADS * HEAD_SIZE
TILE = 1024
LANES = 128
MIB = 1024 * 1024
CHUNKS = ((2, 4), (0, 2))


def bit_reverse(position, count):
    result = 0
    while count > 1:
        result = result * 2 + position % 2
        position //= 2
        count //= 2
    return result


def projection_kernel(
    count, rows, tiles, with_squares,
    me_ref, acts_ref, gain_ref, w_ref, send_ref, keep_ref, wide, scaled,
):
    step = pl.program_id(0)
    half = count * rows // 2
    me = me_ref[0]

    @pl.when(step == 0)
    def _():
        wide[...] = acts_ref[...].astype(jnp.float32)
        gain = gain_ref[...].astype(jnp.float32)
        for pair in range(count // 2):
            parts = []
            for position in (2 * pair, 2 * pair + 1):
                source = jnp.bitwise_xor(me, bit_reverse(position, count))
                start = pl.multiple_of(source * rows, rows)
                parts.append(wide[pl.ds(start, rows), :])
            both = jnp.concatenate(parts, axis=0)
            where = pl.ds(2 * pair * rows, 2 * rows)
            scaled[where, :] = (both * gain).astype(jnp.bfloat16)
            if with_squares:
                squares = jnp.sum(both * both, axis=1, keepdims=True)
                high = squares.astype(jnp.bfloat16).astype(jnp.float32)
                lane = lax.broadcasted_iota(jnp.int32, (2 * rows, LANES), 1)
                lanes = jnp.where(lane == 2 * me, high, 0.0)
                lanes = jnp.where(lane == 2 * me + 1, squares - high, lanes)
                if 2 * pair < count // 2:
                    keep_ref[where, tiles * TILE :] = lanes
                else:
                    send_ref[pl.ds(2 * pair * rows - half, 2 * rows), tiles * TILE :] = (
                        lanes.astype(jnp.bfloat16)
                    )

    product = jnp.dot(scaled[...], w_ref[...], preferred_element_type=jnp.float32)
    columns = pl.ds(pl.multiple_of(step * TILE, TILE), TILE)
    keep_ref[:, columns] = product[:half]
    send_ref[:, columns] = product[half:].astype(jnp.bfloat16)


def project(me, activations, gain, w_qkv, count, rows, start, width, with_squares):
    tiles = width // TILE
    depth = w_qkv.shape[0]
    half = count * rows // 2
    whole = width + (LANES if with_squares else 0)
    return pl.pallas_call(
        functools.partial(projection_kernel, count, rows, tiles, with_squares),
        grid_spec=pltpu.PrefetchScalarGridSpec(
            num_scalar_prefetch=1,
            grid=(tiles,),
            in_specs=[
                pl.BlockSpec(activations.shape, lambda j, me: (0, 0)),
                pl.BlockSpec((1, depth), lambda j, me: (0, 0)),
                pl.BlockSpec((depth, TILE), lambda j, me: (0, start // TILE + j)),
            ],
            out_specs=[
                pl.BlockSpec((half, whole), lambda j, me: (0, 0)),
                pl.BlockSpec((half, whole), lambda j, me: (0, 0)),
            ],
            scratch_shapes=[
                pltpu.VMEM(activations.shape, jnp.float32),
                pltpu.VMEM(activations.shape, jnp.bfloat16),
            ],
        ),
        out_shape=[
            jax.ShapeDtypeStruct((half, whole), jnp.bfloat16),
            jax.ShapeDtypeStruct((half, whole), jnp.float32),
        ],
        compiler_params=pltpu.CompilerParams(vmem_limit_bytes=32 * MIB),
        cost_estimate=pl.CostEstimate(
            flops=4 * half * depth * width,
            bytes_accessed=2 * depth * width + 6 * half * whole,
            transcendentals=0,
        ),
    )(me, activations, gain, w_qkv)


def output_kernel(
    count, rows, tiles, first, last, me_ref, *refs
):
    mine_ref, other_ref, w_ref = refs[:3]
    refs = refs[3:]
    if not first:
        before_ref, refs = refs[0], refs[1:]
    out_ref, total = refs[0], refs[1]
    step = pl.program_id(0)
    columns = pl.ds(pl.multiple_of(step * TILE, TILE), TILE)
    left = jnp.concatenate([mine_ref[:, columns], other_ref[:, columns]], axis=0)
    product = jnp.dot(left, w_ref[...], preferred_element_type=jnp.float32)

    @pl.when(step == 0)
    def _():
        total[...] = product if first else before_ref[...] + product

    @pl.when(step > 0)
    def _():
        total[...] += product

    @pl.when(step == tiles - 1)
    def _():
        if not last:
            out_ref[...] = total[...]
            return
        reversed_me = me_ref[1]
        for pair in range(count // 2):
            parts = []
            for block in (2 * pair, 2 * pair + 1):
                reversed_block = bit_reverse(block, count)
                position = jnp.bitwise_xor(reversed_me, reversed_block)
                parts.append(total[pl.ds(pl.multiple_of(position * rows, rows), rows), :])
            out_ref[pl.ds(2 * pair * rows, 2 * rows), :] = jnp.concatenate(
                parts, axis=0
            ).astype(jnp.bfloat16)


def output_part(me, mine, other, w_out, before, count, rows, start, last):
    width = mine.shape[1]
    tiles = width // TILE
    columns = w_out.shape[1]
    whole = lambda j, me: (0, 0)
    in_specs = [
        pl.BlockSpec(mine.shape, whole),
        pl.BlockSpec(other.shape, whole),
        pl.BlockSpec((TILE, columns), lambda j, me: (start // TILE + j, 0)),
    ]
    operands = [mine, other, w_out]
    first = before is None
    if not first:
        in_specs.append(pl.BlockSpec(before.shape, whole))
        operands.append(before)
    shape = (count * rows, columns)
    return pl.pallas_call(
        functools.partial(output_kernel, count, rows, tiles, first, last),
        grid_spec=pltpu.PrefetchScalarGridSpec(
            num_scalar_prefetch=1,
            grid=(tiles,),
            in_specs=in_specs,
            out_specs=pl.BlockSpec(shape, whole),
            scratch_shapes=[pltpu.VMEM(shape, jnp.float32)],
        ),
        out_shape=jax.ShapeDtypeStruct(shape, jnp.bfloat16 if last else jnp.float32),
        compiler_params=pltpu.CompilerParams(vmem_limit_bytes=32 * MIB),
        cost_estimate=pl.CostEstimate(
            flops=2 * shape[0] * width * columns,
            bytes_accessed=2 * width * columns + 2 * shape[0] * (width + columns),
            transcendentals=0,
        ),
    )(me, *operands)


def rotation():
    half_dim = HEAD_SIZE // 2
    frequency = jnp.float32(500000.0) ** (
        -jnp.arange(half_dim, dtype=jnp.float32) * 2.0 / HEAD_SIZE
    )
    angles = jnp.float32(CONTEXT_LENGTH) * frequency
    return jnp.cos(angles), jnp.sin(angles)


def apply_rotary(tensor):
    half_dim = HEAD_SIZE // 2
    cosine, sine_part = rotation()
    first_half = tensor[..., :half_dim]
    second_half = tensor[..., half_dim:]
    return jnp.concatenate(
        [
            first_half * cosine - second_half * sine_part,
            second_half * cosine + first_half * sine_part,
        ],
        axis=-1,
    )


def attend(query_rows, fresh_keys, fresh_values, cache_keys, value_cache_rows):
    count_of_rows, heads = fresh_keys.shape[:2]
    grouped_queries = query_rows.reshape(count_of_rows, heads, GROUP, HEAD_SIZE)
    scaling = 1.0 / jnp.sqrt(jnp.float32(HEAD_SIZE))
    cached_scores = (
        jnp.einsum(
            "rkgd,rtkd->rkgt", grouped_queries, cache_keys, preferred_element_type=jnp.float32
        )
        * scaling
    )
    own_scores = (
        jnp.einsum("rkgd,rkd->rkg", grouped_queries, fresh_keys, preferred_element_type=jnp.float32)
        * scaling
    )
    highest = jnp.maximum(jnp.max(cached_scores, axis=-1), own_scores)
    cached_exp = jnp.exp(cached_scores - highest[..., None])
    own_exp = jnp.exp(own_scores - highest)
    denominator = jnp.sum(cached_exp, axis=-1) + own_exp
    cached_weights = (cached_exp / denominator[..., None]).astype(jnp.bfloat16)
    own_weights = (own_exp / denominator).astype(jnp.bfloat16)
    combined = jnp.einsum(
        "rkgt,rtkd->rkgd", cached_weights, value_cache_rows, preferred_element_type=jnp.float32
    )
    combined = (
        combined
        + own_weights.astype(jnp.float32)[..., None]
        * fresh_values.astype(jnp.float32)[:, :, None, :]
    )
    return combined.reshape(count_of_rows, heads * GROUP * HEAD_SIZE).astype(jnp.bfloat16)


def swap(value, count, bit):
    return lax.ppermute(value, "gx", [(i, i ^ bit) for i in range(count)])


def reduce_rows(send, keep, count, rows):
    size, bit = count // 2, 1
    received = [swap(send, count, bit)]
    while size > 1:
        size, bit = size // 2, bit * 2
        part = slice(size * rows, 2 * size * rows)
        total = keep[part]
        for piece in received:
            total = total + piece[part].astype(jnp.float32)
        received.append(swap(total.astype(jnp.bfloat16), count, bit))
    total = keep[:rows]
    for piece in received:
        total = total + piece[:rows].astype(jnp.float32)
    return total


def gather_rows(own, count):
    bit = count // 2
    mine = own
    while bit > 1:
        mine = jnp.concatenate([mine, swap(mine, count, bit)], axis=0)
        bit //= 2
    return mine, swap(mine, count, 1)


def body(count, activations, norm_gain, w_qkv, w_out, cache_keys, value_cache_rows):
    rows = cache_keys.shape[0]
    index = lax.axis_index("gx").astype(jnp.int32)
    reversed_index = jnp.int32(0)
    bit = 1
    while bit < count:
        reversed_index = reversed_index * 2 + (index // bit) % 2
        bit *= 2
    me = jnp.stack([index, reversed_index])
    gain = norm_gain[None, :]
    per_head = GROUP * HEAD_SIZE

    sums = []
    for order, (low, high) in enumerate(CHUNKS):
        first = order == 0
        start = low * per_head
        width = (QKVW if first else high * per_head) - start
        send, keep = project(
            me, activations, gain, w_qkv, count, rows, start, width, first
        )
        sums.append(reduce_rows(send, keep, count, rows))

    lead = sums[0]
    width = (CHUNKS[0][1] - CHUNKS[0][0]) * per_head
    own_squares = jnp.sum(lead[:, -LANES:], axis=1)
    inverse_rms = lax.rsqrt(own_squares / D + 1e-05)[:, None]
    fresh = lead[:, width:-LANES] * inverse_rms
    kv_width = KEY_VALUE_HEADS * HEAD_SIZE
    shape = (rows, KEY_VALUE_HEADS, HEAD_SIZE)
    fresh_keys = apply_rotary(fresh[:, :kv_width].reshape(shape)).astype(jnp.bfloat16)
    fresh_values = fresh[:, kv_width:].reshape(shape).astype(jnp.bfloat16)

    total = None
    for order, (low, high) in enumerate(CHUNKS):
        width = (high - low) * per_head
        queries = apply_rotary(
            (sums[order][:, :width] * inverse_rms).reshape(rows, width // HEAD_SIZE, HEAD_SIZE)
        ).astype(jnp.bfloat16)
        attended = attend(
            queries,
            fresh_keys[:, low:high],
            fresh_values[:, low:high],
            cache_keys[:, :, low:high],
            value_cache_rows[:, :, low:high],
        )
        mine, other = gather_rows(attended, count)
        total = output_part(
            me, mine, other, w_out, total, count, rows, low * per_head,
            order == len(CHUNKS) - 1,
        )
    return total


def solution(mesh):
    return jax.shard_map(
        functools.partial(body, mesh.shape["gx"]),
        mesh=mesh,
        in_specs=(
            P("groups", "gx"),
            P("gx"),
            P("gx", None),
            P(None, "gx"),
            P(("groups", "gx"), None, None, None),
            P(("groups", "gx"), None, None, None),
        ),
        out_specs=P("groups", "gx"),
        check_vma=False,
    )
```

```python
import functools

import jax
import jax.numpy as jnp
from jax import lax
from jax.experimental import pallas as pl
from jax.experimental.pallas import tpu as pltpu
from jax.sharding import PartitionSpec as P

D = 16384
QUERY_HEADS = 64
KEY_VALUE_HEADS = 4
HEAD_SIZE = 128
CONTEXT_LENGTH = 256
GROUP = QUERY_HEADS // KEY_VALUE_HEADS
QUERY_WIDTH = QUERY_HEADS * HEAD_SIZE
QKVW = QUERY_WIDTH + 2 * KEY_VALUE_HEADS * HEAD_SIZE
TILE = 1024
LANES = 128
MIB = 1024 * 1024
CHUNKS = ((2, 4), (0, 2))


def stage_bits(count, order):
    bits = []
    bit = 1
    while bit < count:
        bits.append(bit)
        bit *= 2
    if order % 2 and len(bits) > 2:
        bits = bits[:1] + bits[2:] + bits[1:2]
    return bits


def relative(position, count, bits):
    result, size = 0, count
    for bit in bits:
        size //= 2
        if position & size:
            result |= bit
    return result


def position_of(index, count, bits):
    result, size = 0, count
    for bit in bits:
        size //= 2
        shift = bit.bit_length() - 1
        result = result | ((index >> shift) & 1) * size
    return result


def projection_kernel(
    count, rows, bits, tiles, with_squares,
    me_ref, acts_ref, gain_ref, w_ref, send_ref, keep_ref, wide, scaled,
):
    step = pl.program_id(0)
    half = count * rows // 2
    me = me_ref[0]

    @pl.when(step == 0)
    def _():
        wide[...] = acts_ref[...].astype(jnp.float32)
        gain = gain_ref[...].astype(jnp.float32)
        for pair in range(count // 2):
            parts = []
            for position in (2 * pair, 2 * pair + 1):
                source = jnp.bitwise_xor(me, relative(position, count, bits))
                start = pl.multiple_of(source * rows, rows)
                parts.append(wide[pl.ds(start, rows), :])
            both = jnp.concatenate(parts, axis=0)
            where = pl.ds(2 * pair * rows, 2 * rows)
            scaled[where, :] = (both * gain).astype(jnp.bfloat16)
            if with_squares:
                squares = jnp.sum(both * both, axis=1, keepdims=True)
                high = squares.astype(jnp.bfloat16).astype(jnp.float32)
                lane = lax.broadcasted_iota(jnp.int32, (2 * rows, LANES), 1)
                lanes = jnp.where(lane == 2 * me, high, 0.0)
                lanes = jnp.where(lane == 2 * me + 1, squares - high, lanes)
                if 2 * pair < count // 2:
                    keep_ref[where, tiles * TILE :] = lanes
                else:
                    send_ref[pl.ds(2 * pair * rows - half, 2 * rows), tiles * TILE :] = (
                        lanes.astype(jnp.bfloat16)
                    )

    product = jnp.dot(scaled[...], w_ref[...], preferred_element_type=jnp.float32)
    columns = pl.ds(pl.multiple_of(step * TILE, TILE), TILE)
    keep_ref[:, columns] = product[:half]
    send_ref[:, columns] = product[half:].astype(jnp.bfloat16)


def project(me, activations, gain, w_qkv, count, rows, bits, start, width, with_squares):
    tiles = width // TILE
    depth = w_qkv.shape[0]
    half = count * rows // 2
    whole = width + (LANES if with_squares else 0)
    return pl.pallas_call(
        functools.partial(projection_kernel, count, rows, bits, tiles, with_squares),
        grid_spec=pltpu.PrefetchScalarGridSpec(
            num_scalar_prefetch=1,
            grid=(tiles,),
            in_specs=[
                pl.BlockSpec(activations.shape, lambda j, me: (0, 0)),
                pl.BlockSpec((1, depth), lambda j, me: (0, 0)),
                pl.BlockSpec((depth, TILE), lambda j, me: (0, start // TILE + j)),
            ],
            out_specs=[
                pl.BlockSpec((half, whole), lambda j, me: (0, 0)),
                pl.BlockSpec((half, whole), lambda j, me: (0, 0)),
            ],
            scratch_shapes=[
                pltpu.VMEM(activations.shape, jnp.float32),
                pltpu.VMEM(activations.shape, jnp.bfloat16),
            ],
        ),
        out_shape=[
            jax.ShapeDtypeStruct((half, whole), jnp.bfloat16),
            jax.ShapeDtypeStruct((half, whole), jnp.float32),
        ],
        compiler_params=pltpu.CompilerParams(vmem_limit_bytes=20 * MIB),
        cost_estimate=pl.CostEstimate(
            flops=4 * half * depth * width,
            bytes_accessed=2 * depth * width + 6 * half * whole,
            transcendentals=0,
        ),
    )(me, activations, gain, w_qkv)


def output_kernel(count, rows, bits, tiles, first, last, me_ref, *refs):
    mine_ref, other_ref, w_ref = refs[:3]
    out_ref, total = refs[-2:]
    step = pl.program_id(0)
    columns = pl.ds(pl.multiple_of(step * TILE, TILE), TILE)
    left = jnp.concatenate([mine_ref[:, columns], other_ref[:, columns]], axis=0)
    product = jnp.dot(left, w_ref[...], preferred_element_type=jnp.float32)

    @pl.when(step == 0)
    def _():
        total[...] = product

    @pl.when(step > 0)
    def _():
        total[...] += product

    @pl.when(step == tiles - 1)
    def _():
        mine = position_of(me_ref[0], count, bits)
        for pair in range(count // 2):
            parts = []
            for block in (2 * pair, 2 * pair + 1):
                position = jnp.bitwise_xor(mine, position_of(block, count, bits))
                parts.append(total[pl.ds(pl.multiple_of(position * rows, rows), rows), :])
            both = jnp.concatenate(parts, axis=0)
            where = pl.ds(2 * pair * rows, 2 * rows)
            if not first:
                both += refs[3][where, :]
            out_ref[where, :] = both.astype(out_ref.dtype)


def output_part(me, mine, other, w_out, before, count, rows, bits, start, last):
    width = mine.shape[1]
    tiles = width // TILE
    columns = w_out.shape[1]
    whole = lambda j, me: (0, 0)
    in_specs = [
        pl.BlockSpec(mine.shape, whole),
        pl.BlockSpec(other.shape, whole),
        pl.BlockSpec((TILE, columns), lambda j, me: (start // TILE + j, 0)),
    ]
    operands = [mine, other, w_out]
    first = before is None
    if not first:
        in_specs.append(pl.BlockSpec(before.shape, whole))
        operands.append(before)
    shape = (count * rows, columns)
    return pl.pallas_call(
        functools.partial(output_kernel, count, rows, bits, tiles, first, last),
        grid_spec=pltpu.PrefetchScalarGridSpec(
            num_scalar_prefetch=1,
            grid=(tiles,),
            in_specs=in_specs,
            out_specs=pl.BlockSpec(shape, whole),
            scratch_shapes=[pltpu.VMEM(shape, jnp.float32)],
        ),
        out_shape=jax.ShapeDtypeStruct(shape, jnp.bfloat16 if last else jnp.float32),
        compiler_params=pltpu.CompilerParams(vmem_limit_bytes=20 * MIB),
        cost_estimate=pl.CostEstimate(
            flops=2 * shape[0] * width * columns,
            bytes_accessed=2 * width * columns + 2 * shape[0] * (width + columns),
            transcendentals=0,
        ),
    )(me, *operands)


def rotation():
    half_dim = HEAD_SIZE // 2
    frequency = jnp.float32(500000.0) ** (
        -jnp.arange(half_dim, dtype=jnp.float32) * 2.0 / HEAD_SIZE
    )
    angles = jnp.float32(CONTEXT_LENGTH) * frequency
    return jnp.cos(angles), jnp.sin(angles)


def apply_rotary(tensor):
    half_dim = HEAD_SIZE // 2
    cosine, sine_part = rotation()
    first_half = tensor[..., :half_dim]
    second_half = tensor[..., half_dim:]
    return jnp.concatenate(
        [
            first_half * cosine - second_half * sine_part,
            second_half * cosine + first_half * sine_part,
        ],
        axis=-1,
    )


def attend(query_rows, fresh_keys, fresh_values, cache_keys, value_cache_rows):
    count_of_rows, heads = fresh_keys.shape[:2]
    grouped_queries = query_rows.reshape(count_of_rows, heads, GROUP, HEAD_SIZE)
    scaling = 1.0 / jnp.sqrt(jnp.float32(HEAD_SIZE))
    cached_scores = (
        jnp.einsum(
            "rkgd,rtkd->rkgt", grouped_queries, cache_keys, preferred_element_type=jnp.float32
        )
        * scaling
    )
    own_scores = (
        jnp.einsum("rkgd,rkd->rkg", grouped_queries, fresh_keys, preferred_element_type=jnp.float32)
        * scaling
    )
    highest = jnp.maximum(jnp.max(cached_scores, axis=-1), own_scores)
    cached_exp = jnp.exp(cached_scores - highest[..., None])
    own_exp = jnp.exp(own_scores - highest)
    denominator = jnp.sum(cached_exp, axis=-1) + own_exp
    cached_weights = (cached_exp / denominator[..., None]).astype(jnp.bfloat16)
    own_weights = (own_exp / denominator).astype(jnp.bfloat16)
    combined = jnp.einsum(
        "rkgt,rtkd->rkgd", cached_weights, value_cache_rows, preferred_element_type=jnp.float32
    )
    combined = (
        combined
        + own_weights.astype(jnp.float32)[..., None]
        * fresh_values.astype(jnp.float32)[:, :, None, :]
    )
    return combined.reshape(count_of_rows, heads * GROUP * HEAD_SIZE).astype(jnp.bfloat16)


def swap(value, count, bit):
    return lax.ppermute(value, "gx", [(i, i ^ bit) for i in range(count)])


def reduce_rows(send, keep, count, rows, bits):
    size = count // 2
    received = [swap(send, count, bits[0])]
    for bit in bits[1:]:
        size //= 2
        part = slice(size * rows, 2 * size * rows)
        total = keep[part]
        for piece in received:
            total = total + piece[part].astype(jnp.float32)
        received.append(swap(total.astype(jnp.bfloat16), count, bit))
    total = keep[:rows]
    for piece in received:
        total = total + piece[:rows].astype(jnp.float32)
    return total


def gather_rows(own, count, bits):
    mine = own
    for bit in bits[:0:-1]:
        mine = jnp.concatenate([mine, swap(mine, count, bit)], axis=0)
    return mine, swap(mine, count, bits[0])


def body(count, activations, norm_gain, w_qkv, w_out, cache_keys, value_cache_rows):
    rows = cache_keys.shape[0]
    me = lax.axis_index("gx").astype(jnp.int32)[None]
    w_qkv = pltpu.with_memory_space_constraint(w_qkv, pltpu.HBM)
    gain = norm_gain[None, :]
    per_head = GROUP * HEAD_SIZE

    sums = []
    for order, (low, high) in enumerate(CHUNKS):
        first = order == 0
        bits = stage_bits(count, order)
        start = low * per_head
        width = (QKVW if first else high * per_head) - start
        send, keep = project(
            me, activations, gain, w_qkv, count, rows, bits, start, width, first
        )
        if order == len(CHUNKS) - 1:
            w_out, send = lax.optimization_barrier((w_out, send))
        sums.append(reduce_rows(send, keep, count, rows, bits))

    lead = sums[0]
    width = (CHUNKS[0][1] - CHUNKS[0][0]) * per_head
    own_squares = jnp.sum(lead[:, -LANES:], axis=1)
    inverse_rms = lax.rsqrt(own_squares / D + 1e-05)[:, None]
    fresh = lead[:, width:-LANES] * inverse_rms
    kv_width = KEY_VALUE_HEADS * HEAD_SIZE
    shape = (rows, KEY_VALUE_HEADS, HEAD_SIZE)
    fresh_keys = apply_rotary(fresh[:, :kv_width].reshape(shape)).astype(jnp.bfloat16)
    fresh_values = fresh[:, kv_width:].reshape(shape).astype(jnp.bfloat16)

    total = None
    for order, (low, high) in enumerate(CHUNKS):
        width = (high - low) * per_head
        queries = apply_rotary(
            (sums[order][:, :width] * inverse_rms).reshape(rows, width // HEAD_SIZE, HEAD_SIZE)
        ).astype(jnp.bfloat16)
        attended = attend(
            queries,
            fresh_keys[:, low:high],
            fresh_values[:, low:high],
            cache_keys[:, :, low:high],
            value_cache_rows[:, :, low:high],
        )
        bits = stage_bits(count, order)
        mine, other = gather_rows(attended, count, bits)
        total = output_part(
            me, mine, other, w_out, total, count, rows, bits, low * per_head,
            order == len(CHUNKS) - 1,
        )
    return total


def solution(mesh):
    return jax.shard_map(
        functools.partial(body, mesh.shape["gx"]),
        mesh=mesh,
        in_specs=(
            P("groups", "gx"),
            P("gx"),
            P("gx", None),
            P(None, "gx"),
            P(("groups", "gx"), None, None, None),
            P(("groups", "gx"), None, None, None),
        ),
        out_specs=P("groups", "gx"),
        check_vma=False,
    )
```

```python
import functools

import jax
import jax.numpy as jnp
from jax import lax
from jax.experimental import pallas as pl
from jax.experimental.pallas import tpu as pltpu
from jax.sharding import PartitionSpec as P

D = 16384
QUERY_HEADS = 64
KEY_VALUE_HEADS = 4
HEAD_SIZE = 128
CONTEXT_LENGTH = 256
GROUP = QUERY_HEADS // KEY_VALUE_HEADS
QUERY_WIDTH = QUERY_HEADS * HEAD_SIZE
QKVW = QUERY_WIDTH + 2 * KEY_VALUE_HEADS * HEAD_SIZE
TILE = 1024
LANES = 128
MIB = 1024 * 1024
CHUNKS = ((2, 4), (0, 2))


def stage_bits(count):
    bits = []
    bit = 2
    while bit < count:
        bits.append(bit)
        bit *= 2
    return bits, bits[1:] + bits[:1]


def place(index, count, order):
    result, size = 0, count // 2
    for bit in stage_bits(count)[order]:
        size //= 2
        result = result | ((index >> (bit.bit_length() - 1)) & 1) * size
    return result


def places(me, count):
    own = [place(me, count, order) for order in range(2)]
    core = me & 1
    result = []
    for block in range(count):
        order = block & 1
        half = jnp.bitwise_xor(core, order) * (count // 2)
        result.append(half + jnp.bitwise_xor(own[order], place(block, count, order)))
    return result


def fetch(w_ref, weights, sems, start, tiles):
    copies = [
        pltpu.make_async_copy(
            w_ref.at[:, pl.ds(start + tile * TILE, TILE)], weights.at[tile], sems.at[tile]
        )
        for tile in range(tiles)
    ]
    return copies


def multiply(copies, scaled, weights, send_ref, keep_ref):
    half = keep_ref.shape[0]
    for tile, copy in enumerate(copies):
        copy.wait()
        product = jnp.dot(scaled[...], weights[tile], preferred_element_type=jnp.float32)
        columns = slice(tile * TILE, (tile + 1) * TILE)
        keep_ref[:, columns] = product[:half]
        send_ref[:, columns] = product[half:].astype(jnp.bfloat16)


def first_kernel(
    count, rows, start, width,
    me_ref, acts_ref, gain_ref, w_ref, send_ref, keep_ref, scaled,
    narrow, gains, ordered, squares, weights, small_sems, sems,
):
    half = count * rows // 2
    me = me_ref[0]
    small = [
        pltpu.make_async_copy(acts_ref, narrow, small_sems.at[0]),
        pltpu.make_async_copy(gain_ref, gains, small_sems.at[1]),
    ]
    copies = fetch(w_ref, weights, sems, start, width // TILE)
    for copy in small + copies:
        copy.start()
    for copy in small:
        copy.wait()
    gain = gains[...].astype(jnp.float32)[None, :]
    lane = lax.broadcasted_iota(jnp.int32, (rows, LANES), 1)
    targets = places(me, count)
    for pair in range(count // 2):
        both = narrow[2 * pair * rows : 2 * (pair + 1) * rows, :].astype(jnp.float32)
        for side in range(2):
            wide = both[side * rows : (side + 1) * rows]
            target = targets[2 * pair + side]
            where = pl.ds(pl.multiple_of(target * rows, rows), rows)
            ordered[where, :] = wide * gain
            total = jnp.sum(wide * wide, axis=1, keepdims=True)
            high = total.astype(jnp.bfloat16).astype(jnp.float32)
            lanes = jnp.where(lane == 2 * me, high, 0.0)
            squares[where, :] = jnp.where(lane == 2 * me + 1, total - high, lanes)
    scaled[...] = ordered[...].astype(jnp.bfloat16)
    keep_ref[:, width:] = squares[:half]
    send_ref[:, width:] = squares[half:].astype(jnp.bfloat16)
    multiply(copies, scaled, weights, send_ref, keep_ref)


def later_kernel(start, width, scaled, w_ref, send_ref, keep_ref, weights, sems):
    copies = fetch(w_ref, weights, sems, start, width // TILE)
    for copy in copies:
        copy.start()
    multiply(copies, scaled, weights, send_ref, keep_ref)


def project(me, activations, gain, w_qkv, scaled, count, rows, start, width):
    tiles = width // TILE
    depth = w_qkv.shape[0]
    half = count * rows // 2
    first = scaled is None
    whole = width + (LANES if first else 0)
    in_hbm = pl.BlockSpec(memory_space=pltpu.HBM)
    in_vmem = pl.BlockSpec(memory_space=pltpu.VMEM)
    out_shape = [
        jax.ShapeDtypeStruct((half, whole), jnp.bfloat16),
        jax.ShapeDtypeStruct((half, whole), jnp.float32),
    ]
    scratch = [
        pltpu.VMEM((tiles, depth, TILE), jnp.bfloat16),
        pltpu.SemaphoreType.DMA((tiles,)),
    ]
    if first:
        kernel = functools.partial(first_kernel, count, rows, start, width)
        operands = (me, activations, gain, w_qkv)
        in_specs = [pl.BlockSpec(memory_space=pltpu.SMEM)] + [in_hbm] * 3
        out_shape.append(jax.ShapeDtypeStruct(activations.shape, jnp.bfloat16))
        scratch = [
            pltpu.VMEM(activations.shape, jnp.bfloat16),
            pltpu.VMEM(gain.shape, jnp.bfloat16),
            pltpu.VMEM(activations.shape, jnp.float32),
            pltpu.VMEM((2 * half, LANES), jnp.float32),
            scratch[0],
            pltpu.SemaphoreType.DMA((2,)),
            scratch[1],
        ]
    else:
        kernel = functools.partial(later_kernel, start, width)
        operands = (scaled, w_qkv)
        in_specs = [in_vmem, in_hbm]
    return pl.pallas_call(
        kernel,
        in_specs=in_specs,
        out_specs=[in_vmem] * len(out_shape),
        scratch_shapes=scratch,
        out_shape=out_shape,
        compiler_params=pltpu.CompilerParams(vmem_limit_bytes=24 * MIB),
        cost_estimate=pl.CostEstimate(
            flops=4 * half * depth * width,
            bytes_accessed=2 * depth * width + 6 * half * whole,
            transcendentals=0,
        ),
    )(*operands)


def output_kernel(count, rows, tiles, first, me_ref, *refs):
    mine_ref, other_ref, w_ref = refs[:3]
    out_ref, total = refs[-2:]
    step = pl.program_id(0)
    columns = pl.ds(pl.multiple_of(step * TILE, TILE), TILE)
    left = jnp.concatenate([mine_ref[:, columns], other_ref[:, columns]], axis=0)
    product = jnp.dot(left, w_ref[...], preferred_element_type=jnp.float32)

    @pl.when(step == 0)
    def _():
        total[...] = product if first else refs[3][...] + product

    @pl.when(step > 0)
    def _():
        total[...] += product

    @pl.when(step == tiles - 1)
    def _():
        if out_ref.dtype == jnp.float32:
            out_ref[...] = total[...]
            return
        sources = places(me_ref[0], count)
        for pair in range(count // 2):
            parts = []
            for source in sources[2 * pair : 2 * pair + 2]:
                parts.append(total[pl.ds(pl.multiple_of(source * rows, rows), rows), :])
            where = slice(2 * pair * rows, 2 * (pair + 1) * rows)
            out_ref[where, :] = jnp.concatenate(parts, axis=0).astype(out_ref.dtype)


def output_part(me, mine, other, w_out, before, count, rows, start, last):
    width = mine.shape[1]
    tiles = width // TILE
    columns = w_out.shape[1]
    whole = lambda j, me: (0, 0)
    in_specs = [
        pl.BlockSpec(mine.shape, whole),
        pl.BlockSpec(other.shape, whole),
        pl.BlockSpec((TILE, columns), lambda j, me: (start // TILE + j, 0)),
    ]
    operands = [mine, other, w_out]
    first = before is None
    if not first:
        in_specs.append(pl.BlockSpec(before.shape, whole))
        operands.append(before)
    shape = (count * rows, columns)
    return pl.pallas_call(
        functools.partial(output_kernel, count, rows, tiles, first),
        grid_spec=pltpu.PrefetchScalarGridSpec(
            num_scalar_prefetch=1,
            grid=(tiles,),
            in_specs=in_specs,
            out_specs=pl.BlockSpec(shape, whole),
            scratch_shapes=[pltpu.VMEM(shape, jnp.float32)],
        ),
        out_shape=jax.ShapeDtypeStruct(shape, jnp.bfloat16 if last else jnp.float32),
        compiler_params=pltpu.CompilerParams(vmem_limit_bytes=20 * MIB),
        cost_estimate=pl.CostEstimate(
            flops=2 * shape[0] * width * columns,
            bytes_accessed=2 * width * columns + 2 * shape[0] * (width + columns),
            transcendentals=0,
        ),
    )(me, *operands)


def rotation():
    half_dim = HEAD_SIZE // 2
    frequency = jnp.float32(500000.0) ** (
        -jnp.arange(half_dim, dtype=jnp.float32) * 2.0 / HEAD_SIZE
    )
    angles = jnp.float32(CONTEXT_LENGTH) * frequency
    return jnp.cos(angles), jnp.sin(angles)


def apply_rotary(tensor):
    half_dim = HEAD_SIZE // 2
    cosine, sine_part = rotation()
    first_half = tensor[..., :half_dim]
    second_half = tensor[..., half_dim:]
    return jnp.concatenate(
        [
            first_half * cosine - second_half * sine_part,
            second_half * cosine + first_half * sine_part,
        ],
        axis=-1,
    )


def attend(query_rows, fresh_keys, fresh_values, cache_keys, value_cache_rows):
    count_of_rows, heads = fresh_keys.shape[:2]
    grouped_queries = query_rows.reshape(count_of_rows, heads, GROUP, HEAD_SIZE)
    scaling = 1.0 / jnp.sqrt(jnp.float32(HEAD_SIZE))
    cached_scores = (
        jnp.einsum(
            "rkgd,rtkd->rkgt", grouped_queries, cache_keys, preferred_element_type=jnp.float32
        )
        * scaling
    )
    own_scores = (
        jnp.einsum("rkgd,rkd->rkg", grouped_queries, fresh_keys, preferred_element_type=jnp.float32)
        * scaling
    )
    highest = jnp.maximum(jnp.max(cached_scores, axis=-1), own_scores)
    cached_exp = jnp.exp(cached_scores - highest[..., None])
    own_exp = jnp.exp(own_scores - highest)
    denominator = jnp.sum(cached_exp, axis=-1) + own_exp
    cached_weights = (cached_exp / denominator[..., None]).astype(jnp.bfloat16)
    own_weights = (own_exp / denominator).astype(jnp.bfloat16)
    combined = jnp.einsum(
        "rkgt,rtkd->rkgd", cached_weights, value_cache_rows, preferred_element_type=jnp.float32
    )
    combined = (
        combined
        + own_weights.astype(jnp.float32)[..., None]
        * fresh_values.astype(jnp.float32)[:, :, None, :]
    )
    return combined.reshape(count_of_rows, heads * GROUP * HEAD_SIZE).astype(jnp.bfloat16)


def swap(value, count, stage=None):
    orders = stage_bits(count)
    partners = [
        (i, i ^ (1 if stage is None else orders[i & 1][stage])) for i in range(count)
    ]
    return lax.ppermute(value, "gx", partners)


def tie(value, token):
    return lax.optimization_barrier((value, token))[0]


class Reduction:
    def __init__(self, send, keep, count, rows):
        self.keep, self.count, self.rows = keep, count, rows
        self.size = count // 2
        self.received = [swap(send, count)]

    def combine(self, part):
        total = self.keep[part]
        for piece in self.received:
            total = total + piece[part].astype(jnp.float32)
        return total

    def stage(self):
        self.size //= 2
        part = slice(self.size * self.rows, 2 * self.size * self.rows)
        send = self.combine(part).astype(jnp.bfloat16)
        self.received.append(swap(send, self.count, len(self.received) - 1))
        return send

    def own(self):
        return self.combine(slice(0, self.rows))


def gather_rows(own, count):
    mine = own
    for stage in reversed(range(len(stage_bits(count)[0]))):
        mine = jnp.concatenate([mine, swap(mine, count, stage)], axis=0)
    return mine, swap(mine, count)


def body(count, activations, norm_gain, w_qkv, w_out, cache_keys, value_cache_rows):
    rows = cache_keys.shape[0]
    me = lax.axis_index("gx").astype(jnp.int32)[None]
    activations, norm_gain, w_qkv = [
        pltpu.with_memory_space_constraint(value, pltpu.HBM)
        for value in (activations, norm_gain, w_qkv)
    ]
    per_head = GROUP * HEAD_SIZE

    parts = []
    scaled = None
    for order, (low, high) in enumerate(CHUNKS):
        start = low * per_head
        width = (high * per_head if order else QKVW) - start
        send, keep, *rest = project(
            me, activations, norm_gain, w_qkv, scaled, count, rows, start, width
        )
        if order == 0:
            scaled = rest[0]
        parts.append(Reduction(send, keep, count, rows))
    w_out = tie(w_out, send)
    for stage in range(len(stage_bits(count)[0])):
        for part in parts:
            token = part.stage()
        if stage == 0:
            cache_keys = tie(cache_keys, token)
            value_cache_rows = tie(value_cache_rows, token)
    sums = [part.own() for part in parts]

    lead = sums[0]
    width = (CHUNKS[0][1] - CHUNKS[0][0]) * per_head
    own_squares = jnp.sum(lead[:, -LANES:], axis=1)
    inverse_rms = lax.rsqrt(own_squares / D + 1e-05)[:, None]
    fresh = lead[:, width:-LANES] * inverse_rms
    kv_width = KEY_VALUE_HEADS * HEAD_SIZE
    shape = (rows, KEY_VALUE_HEADS, HEAD_SIZE)
    fresh_keys = apply_rotary(fresh[:, :kv_width].reshape(shape)).astype(jnp.bfloat16)
    fresh_values = fresh[:, kv_width:].reshape(shape).astype(jnp.bfloat16)

    total = None
    for order, (low, high) in enumerate(CHUNKS):
        width = (high - low) * per_head
        queries = apply_rotary(
            (sums[order][:, :width] * inverse_rms).reshape(rows, width // HEAD_SIZE, HEAD_SIZE)
        ).astype(jnp.bfloat16)
        attended = attend(
            queries,
            fresh_keys[:, low:high],
            fresh_values[:, low:high],
            cache_keys[:, :, low:high],
            value_cache_rows[:, :, low:high],
        )
        mine, other = gather_rows(attended, count)
        total = output_part(
            me, mine, other, w_out, total, count, rows, low * per_head,
            order == len(CHUNKS) - 1,
        )
    return total


def solution(mesh):
    return jax.shard_map(
        functools.partial(body, mesh.shape["gx"]),
        mesh=mesh,
        in_specs=(
            P("groups", "gx"),
            P("gx"),
            P("gx", None),
            P(None, "gx"),
            P(("groups", "gx"), None, None, None),
            P(("groups", "gx"), None, None, None),
        ),
        out_specs=P("groups", "gx"),
        check_vma=False,
    )
```

```python
import functools

import jax
import jax.numpy as jnp
from jax import lax
from jax.experimental import pallas as pl
from jax.experimental.pallas import tpu as pltpu
from jax.sharding import PartitionSpec as P

D = 16384
QUERY_HEADS = 64
KEY_VALUE_HEADS = 4
HEAD_SIZE = 128
CONTEXT_LENGTH = 256
GROUP = QUERY_HEADS // KEY_VALUE_HEADS
QUERY_WIDTH = QUERY_HEADS * HEAD_SIZE
QKVW = QUERY_WIDTH + 2 * KEY_VALUE_HEADS * HEAD_SIZE
TILE = 1024
ORDERS = ("is", "is")
LANES = 128
MIB = 1024 * 1024
CHUNKS = ((2, 4), (0, 2))


def stage_bits(count, phase):
    bits = []
    bit = 2
    while bit < count:
        bits.append(bit)
        bit *= 2
    swapped = bits[1:2] + bits[:1] + bits[2:]
    rotated = bits[1:] + bits[:1]
    return [{"i": bits, "s": swapped, "r": rotated}[name] for name in ORDERS[phase]]


def place(index, count, phase, order):
    result, size = 0, count // 2
    for bit in stage_bits(count, phase)[order]:
        size //= 2
        result = result | ((index >> (bit.bit_length() - 1)) & 1) * size
    return result


def places(me, count, phase):
    own = [place(me, count, phase, order) for order in range(2)]
    core = me & 1
    result = []
    for block in range(count):
        order = block & 1
        half = jnp.bitwise_xor(core, order) * (count // 2)
        result.append(half + jnp.bitwise_xor(own[order], place(block, count, phase, order)))
    return result


def fetch(w_ref, weights, sems, start, tiles):
    copies = [
        pltpu.make_async_copy(
            w_ref.at[:, pl.ds(start + tile * TILE, TILE)], weights.at[tile], sems.at[tile]
        )
        for tile in range(tiles)
    ]
    return copies


def multiply(copies, scaled, weights, send_ref, keep_ref):
    half = keep_ref.shape[0]
    for tile, copy in enumerate(copies):
        copy.wait()
        product = jnp.dot(scaled[...], weights[tile], preferred_element_type=jnp.float32)
        columns = slice(tile * TILE, (tile + 1) * TILE)
        keep_ref[:, columns] = product[:half]
        send_ref[:, columns] = product[half:].astype(jnp.bfloat16)


def first_kernel(
    count, rows, start, width,
    me_ref, acts_ref, gain_ref, w_ref, send_ref, keep_ref, scaled,
    narrow, gains, ordered, squares, weights, small_sems, sems,
):
    half = count * rows // 2
    me = me_ref[0]
    small = [
        pltpu.make_async_copy(acts_ref, narrow, small_sems.at[0]),
        pltpu.make_async_copy(gain_ref, gains, small_sems.at[1]),
    ]
    copies = fetch(w_ref, weights, sems, start, width // TILE)
    for copy in small + copies:
        copy.start()
    for copy in small:
        copy.wait()
    gain = gains[...].astype(jnp.float32)[None, :]
    lane = lax.broadcasted_iota(jnp.int32, (rows, LANES), 1)
    targets = places(me, count, 0)
    for pair in range(count // 2):
        both = narrow[2 * pair * rows : 2 * (pair + 1) * rows, :].astype(jnp.float32)
        for side in range(2):
            wide = both[side * rows : (side + 1) * rows]
            target = targets[2 * pair + side]
            where = pl.ds(pl.multiple_of(target * rows, rows), rows)
            ordered[where, :] = wide * gain
            total = jnp.sum(wide * wide, axis=1, keepdims=True)
            high = total.astype(jnp.bfloat16).astype(jnp.float32)
            lanes = jnp.where(lane == 2 * me, high, 0.0)
            squares[where, :] = jnp.where(lane == 2 * me + 1, total - high, lanes)
    scaled[...] = ordered[...].astype(jnp.bfloat16)
    keep_ref[:, width:] = squares[:half]
    send_ref[:, width:] = squares[half:].astype(jnp.bfloat16)
    multiply(copies, scaled, weights, send_ref, keep_ref)


def later_kernel(start, width, scaled, w_ref, send_ref, keep_ref, weights, sems):
    copies = fetch(w_ref, weights, sems, start, width // TILE)
    for copy in copies:
        copy.start()
    multiply(copies, scaled, weights, send_ref, keep_ref)


def project(me, activations, gain, w_qkv, scaled, count, rows, start, width):
    tiles = width // TILE
    depth = w_qkv.shape[0]
    half = count * rows // 2
    first = scaled is None
    whole = width + (LANES if first else 0)
    in_hbm = pl.BlockSpec(memory_space=pltpu.HBM)
    in_vmem = pl.BlockSpec(memory_space=pltpu.VMEM)
    out_shape = [
        jax.ShapeDtypeStruct((half, whole), jnp.bfloat16),
        jax.ShapeDtypeStruct((half, whole), jnp.float32),
    ]
    scratch = [
        pltpu.VMEM((tiles, depth, TILE), jnp.bfloat16),
        pltpu.SemaphoreType.DMA((tiles,)),
    ]
    if first:
        kernel = functools.partial(first_kernel, count, rows, start, width)
        operands = (me, activations, gain, w_qkv)
        in_specs = [pl.BlockSpec(memory_space=pltpu.SMEM)] + [in_hbm] * 3
        out_shape.append(jax.ShapeDtypeStruct(activations.shape, jnp.bfloat16))
        scratch = [
            pltpu.VMEM(activations.shape, jnp.bfloat16),
            pltpu.VMEM(gain.shape, jnp.bfloat16),
            pltpu.VMEM(activations.shape, jnp.float32),
            pltpu.VMEM((2 * half, LANES), jnp.float32),
            scratch[0],
            pltpu.SemaphoreType.DMA((2,)),
            scratch[1],
        ]
    else:
        kernel = functools.partial(later_kernel, start, width)
        operands = (scaled, w_qkv)
        in_specs = [in_vmem, in_hbm]
    return pl.pallas_call(
        kernel,
        in_specs=in_specs,
        out_specs=[in_vmem] * len(out_shape),
        scratch_shapes=scratch,
        out_shape=out_shape,
        compiler_params=pltpu.CompilerParams(vmem_limit_bytes=24 * MIB),
        cost_estimate=pl.CostEstimate(
            flops=4 * half * depth * width,
            bytes_accessed=2 * depth * width + 6 * half * whole,
            transcendentals=0,
        ),
    )(*operands)


def output_kernel(count, rows, tiles, first, me_ref, *refs):
    mine_ref, other_ref, w_ref = refs[:3]
    out_ref, total = refs[-2:]
    step = pl.program_id(0)
    columns = pl.ds(pl.multiple_of(step * TILE, TILE), TILE)
    left = jnp.concatenate([mine_ref[:, columns], other_ref[:, columns]], axis=0)
    product = jnp.dot(left, w_ref[...], preferred_element_type=jnp.float32)

    @pl.when(step == 0)
    def _():
        total[...] = product if first else refs[3][...] + product

    @pl.when(step > 0)
    def _():
        total[...] += product

    @pl.when(step == tiles - 1)
    def _():
        if out_ref.dtype == jnp.float32:
            out_ref[...] = total[...]
            return
        sources = places(me_ref[0], count, 1)
        for pair in range(count // 2):
            parts = []
            for source in sources[2 * pair : 2 * pair + 2]:
                parts.append(total[pl.ds(pl.multiple_of(source * rows, rows), rows), :])
            where = slice(2 * pair * rows, 2 * (pair + 1) * rows)
            out_ref[where, :] = jnp.concatenate(parts, axis=0).astype(out_ref.dtype)


def output_part(me, mine, other, w_out, before, count, rows, start, last):
    width = mine.shape[1]
    tiles = width // TILE
    columns = w_out.shape[1]
    whole = lambda j, me: (0, 0)
    in_specs = [
        pl.BlockSpec(mine.shape, whole),
        pl.BlockSpec(other.shape, whole),
        pl.BlockSpec((TILE, columns), lambda j, me: (start // TILE + j, 0)),
    ]
    operands = [mine, other, w_out]
    first = before is None
    if not first:
        in_specs.append(pl.BlockSpec(before.shape, whole))
        operands.append(before)
    shape = (count * rows, columns)
    return pl.pallas_call(
        functools.partial(output_kernel, count, rows, tiles, first),
        grid_spec=pltpu.PrefetchScalarGridSpec(
            num_scalar_prefetch=1,
            grid=(tiles,),
            in_specs=in_specs,
            out_specs=pl.BlockSpec(shape, whole),
            scratch_shapes=[pltpu.VMEM(shape, jnp.float32)],
        ),
        out_shape=jax.ShapeDtypeStruct(shape, jnp.bfloat16 if last else jnp.float32),
        compiler_params=pltpu.CompilerParams(vmem_limit_bytes=20 * MIB),
        cost_estimate=pl.CostEstimate(
            flops=2 * shape[0] * width * columns,
            bytes_accessed=2 * width * columns + 2 * shape[0] * (width + columns),
            transcendentals=0,
        ),
    )(me, *operands)


def rotation():
    half_dim = HEAD_SIZE // 2
    frequency = jnp.float32(500000.0) ** (
        -jnp.arange(half_dim, dtype=jnp.float32) * 2.0 / HEAD_SIZE
    )
    angles = jnp.float32(CONTEXT_LENGTH) * frequency
    return jnp.cos(angles), jnp.sin(angles)


def apply_rotary(tensor):
    half_dim = HEAD_SIZE // 2
    cosine, sine_part = rotation()
    first_half = tensor[..., :half_dim]
    second_half = tensor[..., half_dim:]
    return jnp.concatenate(
        [
            first_half * cosine - second_half * sine_part,
            second_half * cosine + first_half * sine_part,
        ],
        axis=-1,
    )


def attend(query_rows, fresh_keys, fresh_values, cache_keys, value_cache_rows):
    count_of_rows, heads = fresh_keys.shape[:2]
    grouped_queries = query_rows.reshape(count_of_rows, heads, GROUP, HEAD_SIZE)
    scaling = 1.0 / jnp.sqrt(jnp.float32(HEAD_SIZE))
    cached_scores = (
        jnp.einsum(
            "rkgd,rtkd->rkgt", grouped_queries, cache_keys, preferred_element_type=jnp.float32
        )
        * scaling
    )
    own_scores = (
        jnp.einsum("rkgd,rkd->rkg", grouped_queries, fresh_keys, preferred_element_type=jnp.float32)
        * scaling
    )
    highest = jnp.maximum(jnp.max(cached_scores, axis=-1), own_scores)
    cached_exp = jnp.exp(cached_scores - highest[..., None])
    own_exp = jnp.exp(own_scores - highest)
    denominator = jnp.sum(cached_exp, axis=-1) + own_exp
    cached_weights = (cached_exp / denominator[..., None]).astype(jnp.bfloat16)
    own_weights = (own_exp / denominator).astype(jnp.bfloat16)
    combined = jnp.einsum(
        "rkgt,rtkd->rkgd", cached_weights, value_cache_rows, preferred_element_type=jnp.float32
    )
    combined = (
        combined
        + own_weights.astype(jnp.float32)[..., None]
        * fresh_values.astype(jnp.float32)[:, :, None, :]
    )
    return combined.reshape(count_of_rows, heads * GROUP * HEAD_SIZE).astype(jnp.bfloat16)


def swap(value, count, phase=None, stage=None):
    orders = None if phase is None else stage_bits(count, phase)
    partners = [
        (i, i ^ (1 if phase is None else orders[i & 1][stage])) for i in range(count)
    ]
    return lax.ppermute(value, "gx", partners)


def tie(value, token):
    return lax.optimization_barrier((value, token))[0]


class Reduction:
    def __init__(self, send, keep, count, rows):
        self.keep, self.count, self.rows = keep, count, rows
        self.size = count // 2
        self.received = [swap(send, count)]

    def combine(self, part):
        total = self.keep[part]
        for piece in self.received:
            total = total + piece[part].astype(jnp.float32)
        return total

    def stage(self):
        self.size //= 2
        part = slice(self.size * self.rows, 2 * self.size * self.rows)
        send = self.combine(part).astype(jnp.bfloat16)
        self.received.append(swap(send, self.count, 0, len(self.received) - 1))
        return send

    def own(self):
        return self.combine(slice(0, self.rows))


def body(count, activations, norm_gain, w_qkv, w_out, cache_keys, value_cache_rows):
    rows = cache_keys.shape[0]
    me = lax.axis_index("gx").astype(jnp.int32)[None]
    activations, norm_gain, w_qkv = [
        pltpu.with_memory_space_constraint(value, pltpu.HBM)
        for value in (activations, norm_gain, w_qkv)
    ]
    per_head = GROUP * HEAD_SIZE

    parts = []
    scaled = None
    for order, (low, high) in enumerate(CHUNKS):
        start = low * per_head
        width = (high * per_head if order else QKVW) - start
        send, keep, *rest = project(
            me, activations, norm_gain, w_qkv, scaled, count, rows, start, width
        )
        if order == 0:
            scaled = rest[0]
        parts.append(Reduction(send, keep, count, rows))
    w_out = tie(w_out, send)
    stages = len(stage_bits(count, 0)[0])
    for stage in range(stages):
        for part in parts:
            token = part.stage()
        if stage == 0:
            cache_keys = tie(cache_keys, token)
            value_cache_rows = tie(value_cache_rows, token)
    gathered = []
    for order, (low, high) in enumerate(CHUNKS):
        width = (high - low) * per_head
        if order > 0:
            parts[order].keep = tie(parts[order].keep, gathered[-1])
        sums = parts[order].own()
        if order == 0:
            own_squares = jnp.sum(sums[:, -LANES:], axis=1)
            inverse_rms = lax.rsqrt(own_squares / D + 1e-05)[:, None]
            fresh = sums[:, width:-LANES] * inverse_rms
            kv_width = KEY_VALUE_HEADS * HEAD_SIZE
            shape = (rows, KEY_VALUE_HEADS, HEAD_SIZE)
            fresh_keys = apply_rotary(fresh[:, :kv_width].reshape(shape)).astype(jnp.bfloat16)
            fresh_values = fresh[:, kv_width:].reshape(shape).astype(jnp.bfloat16)
        queries = apply_rotary(
            (sums[:, :width] * inverse_rms).reshape(rows, width // HEAD_SIZE, HEAD_SIZE)
        ).astype(jnp.bfloat16)
        gathered.append(
            attend(
                queries,
                fresh_keys[:, low:high],
                fresh_values[:, low:high],
                cache_keys[:, :, low:high],
                value_cache_rows[:, :, low:high],
            )
        )

    for stage in reversed(range(stages)):
        before = None
        for order in range(len(CHUNKS)):
            mine = gathered[order]
            if before is not None:
                mine = tie(mine, before)
            before = mine
            gathered[order] = jnp.concatenate([mine, swap(mine, count, 1, stage)], axis=0)
    total = None
    for order, (low, high) in enumerate(CHUNKS):
        mine = gathered[order]
        other = swap(mine, count)
        total = output_part(
            me, mine, other, w_out, total, count, rows, low * per_head,
            order == len(CHUNKS) - 1,
        )
    return total


def solution(mesh):
    return jax.shard_map(
        functools.partial(body, mesh.shape["gx"]),
        mesh=mesh,
        in_specs=(
            P("groups", "gx"),
            P("gx"),
            P("gx", None),
            P(None, "gx"),
            P(("groups", "gx"), None, None, None),
            P(("groups", "gx"), None, None, None),
        ),
        out_specs=P("groups", "gx"),
        check_vma=False,
    )
```

```python
import functools

import jax
import jax.numpy as jnp
from jax import lax
from jax.experimental import pallas as pl
from jax.experimental.pallas import tpu as pltpu
from jax.sharding import PartitionSpec as P

D = 16384
QUERY_HEADS = 64
KEY_VALUE_HEADS = 4
HEAD_SIZE = 128
CONTEXT_LENGTH = 256
GROUP = QUERY_HEADS // KEY_VALUE_HEADS
QUERY_WIDTH = QUERY_HEADS * HEAD_SIZE
QKVW = QUERY_WIDTH + 2 * KEY_VALUE_HEADS * HEAD_SIZE
TILE = 1024
COLUMNS = 256
ORDERS = ("is", "is")
LANES = 128
MIB = 1024 * 1024
CHUNKS = ((2, 4), (0, 2))


def stage_bits(count, phase):
    bits = []
    bit = 2
    while bit < count:
        bits.append(bit)
        bit *= 2
    swapped = bits[1:2] + bits[:1] + bits[2:]
    rotated = bits[1:] + bits[:1]
    return [{"i": bits, "s": swapped, "r": rotated}[name] for name in ORDERS[phase]]


def place(index, count, phase, order):
    result, size = 0, count // 2
    for bit in stage_bits(count, phase)[order]:
        size //= 2
        result = result | ((index >> (bit.bit_length() - 1)) & 1) * size
    return result


def places(me, count, phase):
    own = [place(me, count, phase, order) for order in range(2)]
    core = me & 1
    result = []
    for block in range(count):
        order = block & 1
        half = jnp.bitwise_xor(core, order) * (count // 2)
        result.append(half + jnp.bitwise_xor(own[order], place(block, count, phase, order)))
    return result


def fetch(w_ref, weights, sems, start, tiles):
    copies = [
        pltpu.make_async_copy(
            w_ref.at[:, pl.ds(start + tile * TILE, TILE)], weights.at[tile], sems.at[tile]
        )
        for tile in range(tiles)
    ]
    return copies


def multiply(copies, scaled, weights, send_ref, keep_ref):
    half = keep_ref.shape[0]
    for tile in range(weights.shape[0]):
        if copies:
            copies[tile].wait()
        product = jnp.dot(scaled[...], weights[tile], preferred_element_type=jnp.float32)
        columns = slice(tile * TILE, (tile + 1) * TILE)
        keep_ref[:, columns] = product[:half]
        send_ref[:, columns] = product[half:].astype(jnp.bfloat16)


def first_kernel(
    count, rows, span, later_span,
    me_ref, acts_ref, gain_ref, w_ref, send_ref, keep_ref, scaled, later_weights,
    narrow, gains, ordered, squares, weights, small_sems, sems, later_sems,
):
    start, width = span
    half = count * rows // 2
    me = me_ref[0]
    small = [
        pltpu.make_async_copy(acts_ref, narrow, small_sems.at[0]),
        pltpu.make_async_copy(gain_ref, gains, small_sems.at[1]),
    ]
    copies = fetch(w_ref, weights, sems, start, width // TILE)
    later = fetch(w_ref, later_weights, later_sems, later_span[0], later_span[1] // TILE)
    for copy in small + copies + later:
        copy.start()
    for copy in small:
        copy.wait()
    gain = gains[...].astype(jnp.float32)[None, :]
    lane = lax.broadcasted_iota(jnp.int32, (rows, LANES), 1)
    targets = places(me, count, 0)
    for pair in range(count // 2):
        both = narrow[2 * pair * rows : 2 * (pair + 1) * rows, :].astype(jnp.float32)
        for side in range(2):
            wide = both[side * rows : (side + 1) * rows]
            target = targets[2 * pair + side]
            where = pl.ds(pl.multiple_of(target * rows, rows), rows)
            ordered[where, :] = wide * gain
            total = jnp.sum(wide * wide, axis=1, keepdims=True)
            high = total.astype(jnp.bfloat16).astype(jnp.float32)
            lanes = jnp.where(lane == 2 * me, high, 0.0)
            squares[where, :] = jnp.where(lane == 2 * me + 1, total - high, lanes)
    scaled[...] = ordered[...].astype(jnp.bfloat16)
    keep_ref[:, width:] = squares[:half]
    send_ref[:, width:] = squares[half:].astype(jnp.bfloat16)
    multiply(copies, scaled, weights, send_ref, keep_ref)
    for copy in later:
        copy.wait()


def later_kernel(scaled, weights, send_ref, keep_ref):
    multiply(None, scaled, weights, send_ref, keep_ref)


def project(me, activations, gain, w_qkv, count, rows, spans):
    depth = w_qkv.shape[0]
    half = count * rows // 2
    in_hbm = pl.BlockSpec(memory_space=pltpu.HBM)
    in_vmem = pl.BlockSpec(memory_space=pltpu.VMEM)

    def call(kernel, in_specs, operands, width, whole, more_out, scratch):
        out_shape = [
            jax.ShapeDtypeStruct((half, whole), jnp.bfloat16),
            jax.ShapeDtypeStruct((half, whole), jnp.float32),
        ] + more_out
        return pl.pallas_call(
            kernel,
            in_specs=in_specs,
            out_specs=[in_vmem] * len(out_shape),
            scratch_shapes=scratch,
            out_shape=out_shape,
            compiler_params=pltpu.CompilerParams(vmem_limit_bytes=28 * MIB),
            cost_estimate=pl.CostEstimate(
                flops=4 * half * depth * width,
                bytes_accessed=2 * depth * width + 6 * half * whole,
                transcendentals=0,
            ),
        )(*operands)

    tiles, later_tiles = [width // TILE for _, width in spans]
    width, later_width = [width for _, width in spans]
    send, keep, scaled, weights = call(
        functools.partial(first_kernel, count, rows, *spans),
        [pl.BlockSpec(memory_space=pltpu.SMEM)] + [in_hbm] * 3,
        (me, activations, gain, w_qkv),
        width,
        width + LANES,
        [
            jax.ShapeDtypeStruct(activations.shape, jnp.bfloat16),
            jax.ShapeDtypeStruct((later_tiles, depth, TILE), jnp.bfloat16),
        ],
        [
            pltpu.VMEM(activations.shape, jnp.bfloat16),
            pltpu.VMEM(gain.shape, jnp.bfloat16),
            pltpu.VMEM(activations.shape, jnp.float32),
            pltpu.VMEM((2 * half, LANES), jnp.float32),
            pltpu.VMEM((tiles, depth, TILE), jnp.bfloat16),
            pltpu.SemaphoreType.DMA((2,)),
            pltpu.SemaphoreType.DMA((tiles,)),
            pltpu.SemaphoreType.DMA((later_tiles,)),
        ],
    )
    later = call(
        later_kernel, [in_vmem] * 2, (scaled, weights), later_width, later_width, [], []
    )
    return (send, keep), later


def output_kernel(count, rows, start, me_ref, mine_ref, other_ref, w_ref, *refs):
    *before, out_ref, total = refs
    depth = mine_ref.shape[1]
    left = jnp.concatenate([mine_ref[...], other_ref[...]], axis=0)
    last = out_ref.dtype != jnp.float32
    width = min(COLUMNS, total.shape[1])
    for column in range(0, total.shape[1], width):
        columns = slice(column, column + width)
        product = jnp.dot(
            left, w_ref[start : start + depth, columns], preferred_element_type=jnp.float32
        )
        for part in before:
            product += part[:, columns]
        if last:
            total[:, columns] = product
        else:
            out_ref[:, columns] = product
    if not last:
        return
    sources = places(me_ref[0], count, 1)
    for pair in range(count // 2):
        parts = []
        for source in sources[2 * pair : 2 * pair + 2]:
            parts.append(total[pl.ds(pl.multiple_of(source * rows, rows), rows), :])
        where = slice(2 * pair * rows, 2 * (pair + 1) * rows)
        out_ref[where, :] = jnp.concatenate(parts, axis=0).astype(out_ref.dtype)


def output_part(me, mine, other, w_out, before, count, rows, start, last):
    depth, columns = mine.shape[1], w_out.shape[1]
    shape = (count * rows, columns)
    operands = (mine, other, w_out) + (() if before is None else (before,))
    in_vmem = pl.BlockSpec(memory_space=pltpu.VMEM)
    return pl.pallas_call(
        functools.partial(output_kernel, count, rows, start),
        in_specs=[pl.BlockSpec(memory_space=pltpu.SMEM)] + [in_vmem] * len(operands),
        out_specs=in_vmem,
        scratch_shapes=[pltpu.VMEM(shape, jnp.float32)],
        out_shape=jax.ShapeDtypeStruct(shape, jnp.bfloat16 if last else jnp.float32),
        compiler_params=pltpu.CompilerParams(vmem_limit_bytes=28 * MIB),
        cost_estimate=pl.CostEstimate(
            flops=2 * shape[0] * depth * columns,
            bytes_accessed=2 * depth * columns + 2 * shape[0] * (depth + columns),
            transcendentals=0,
        ),
    )(me, *operands)


def rotation():
    half_dim = HEAD_SIZE // 2
    frequency = jnp.float32(500000.0) ** (
        -jnp.arange(half_dim, dtype=jnp.float32) * 2.0 / HEAD_SIZE
    )
    angles = jnp.float32(CONTEXT_LENGTH) * frequency
    return jnp.cos(angles), jnp.sin(angles)


def apply_rotary(tensor):
    half_dim = HEAD_SIZE // 2
    cosine, sine_part = rotation()
    first_half = tensor[..., :half_dim]
    second_half = tensor[..., half_dim:]
    return jnp.concatenate(
        [
            first_half * cosine - second_half * sine_part,
            second_half * cosine + first_half * sine_part,
        ],
        axis=-1,
    )


def attend(query_rows, fresh_keys, fresh_values, cache_keys, value_cache_rows):
    count_of_rows, heads = fresh_keys.shape[:2]
    grouped_queries = query_rows.reshape(count_of_rows, heads, GROUP, HEAD_SIZE)
    scaling = 1.0 / jnp.sqrt(jnp.float32(HEAD_SIZE))
    cached_scores = (
        jnp.einsum(
            "rkgd,rtkd->rkgt", grouped_queries, cache_keys, preferred_element_type=jnp.float32
        )
        * scaling
    )
    own_scores = (
        jnp.einsum("rkgd,rkd->rkg", grouped_queries, fresh_keys, preferred_element_type=jnp.float32)
        * scaling
    )
    highest = jnp.maximum(jnp.max(cached_scores, axis=-1), own_scores)
    cached_exp = jnp.exp(cached_scores - highest[..., None])
    own_exp = jnp.exp(own_scores - highest)
    denominator = jnp.sum(cached_exp, axis=-1) + own_exp
    cached_weights = (cached_exp / denominator[..., None]).astype(jnp.bfloat16)
    own_weights = (own_exp / denominator).astype(jnp.bfloat16)
    combined = jnp.einsum(
        "rkgt,rtkd->rkgd", cached_weights, value_cache_rows, preferred_element_type=jnp.float32
    )
    combined = (
        combined
        + own_weights.astype(jnp.float32)[..., None]
        * fresh_values.astype(jnp.float32)[:, :, None, :]
    )
    return combined.reshape(count_of_rows, heads * GROUP * HEAD_SIZE).astype(jnp.bfloat16)


def swap(value, count, phase=None, stage=None):
    orders = None if phase is None else stage_bits(count, phase)
    partners = [
        (i, i ^ (1 if phase is None else orders[i & 1][stage])) for i in range(count)
    ]
    return lax.ppermute(value, "gx", partners)


def tie(value, token):
    return lax.optimization_barrier((value, token))[0]


class Reduction:
    def __init__(self, send, keep, count, rows):
        self.keep, self.count, self.rows = keep, count, rows
        self.size = count // 2
        self.received = [swap(send, count)]

    def combine(self, part):
        total = self.keep[part]
        for piece in self.received:
            total = total + piece[part].astype(jnp.float32)
        return total

    def stage(self):
        self.size //= 2
        part = slice(self.size * self.rows, 2 * self.size * self.rows)
        send = self.combine(part).astype(jnp.bfloat16)
        self.received.append(swap(send, self.count, 0, len(self.received) - 1))
        return send

    def own(self):
        return self.combine(slice(0, self.rows))


def body(count, activations, norm_gain, w_qkv, w_out, cache_keys, value_cache_rows):
    rows = cache_keys.shape[0]
    me = lax.axis_index("gx").astype(jnp.int32)[None]
    activations, norm_gain, w_qkv = [
        pltpu.with_memory_space_constraint(value, pltpu.HBM)
        for value in (activations, norm_gain, w_qkv)
    ]
    per_head = GROUP * HEAD_SIZE

    spans = []
    for order, (low, high) in enumerate(CHUNKS):
        start = low * per_head
        spans.append((start, (high * per_head if order else QKVW) - start))
    parts = []
    for send, keep in project(me, activations, norm_gain, w_qkv, count, rows, spans):
        parts.append(Reduction(send, keep, count, rows))
    w_out = tie(w_out, send)
    stages = len(stage_bits(count, 0)[0])
    for stage in range(stages):
        for part in parts:
            token = part.stage()
        if stage == 0:
            cache_keys = tie(cache_keys, token)
            value_cache_rows = tie(value_cache_rows, token)
    gathered = []
    for order, (low, high) in enumerate(CHUNKS):
        width = (high - low) * per_head
        if order > 0:
            parts[order].keep = tie(parts[order].keep, gathered[-1])
        sums = parts[order].own()
        if order == 0:
            own_squares = jnp.sum(sums[:, -LANES:], axis=1)
            inverse_rms = lax.rsqrt(own_squares / D + 1e-05)[:, None]
            fresh = sums[:, width:-LANES] * inverse_rms
            kv_width = KEY_VALUE_HEADS * HEAD_SIZE
            shape = (rows, KEY_VALUE_HEADS, HEAD_SIZE)
            fresh_keys = apply_rotary(fresh[:, :kv_width].reshape(shape)).astype(jnp.bfloat16)
            fresh_values = fresh[:, kv_width:].reshape(shape).astype(jnp.bfloat16)
        queries = apply_rotary(
            (sums[:, :width] * inverse_rms).reshape(rows, width // HEAD_SIZE, HEAD_SIZE)
        ).astype(jnp.bfloat16)
        gathered.append(
            attend(
                queries,
                fresh_keys[:, low:high],
                fresh_values[:, low:high],
                cache_keys[:, :, low:high],
                value_cache_rows[:, :, low:high],
            )
        )

    for stage in reversed(range(stages)):
        before = None
        for order in range(len(CHUNKS)):
            mine = gathered[order]
            if before is not None:
                mine = tie(mine, before)
            before = mine
            gathered[order] = jnp.concatenate([mine, swap(mine, count, 1, stage)], axis=0)
    total = None
    for order, (low, high) in enumerate(CHUNKS):
        mine = gathered[order]
        other = swap(mine, count)
        total = output_part(
            me, mine, other, w_out, total, count, rows, low * per_head,
            order == len(CHUNKS) - 1,
        )
    return total


def solution(mesh):
    return jax.shard_map(
        functools.partial(body, mesh.shape["gx"]),
        mesh=mesh,
        in_specs=(
            P("groups", "gx"),
            P("gx"),
            P("gx", None),
            P(None, "gx"),
            P(("groups", "gx"), None, None, None),
            P(("groups", "gx"), None, None, None),
        ),
        out_specs=P("groups", "gx"),
        check_vma=False,
    )
```

```python
import functools

import jax
import jax.numpy as jnp
from jax import lax
from jax.experimental import pallas as pl
from jax.experimental.pallas import tpu as pltpu
from jax.sharding import PartitionSpec as P

D = 16384
QUERY_HEADS = 64
KEY_VALUE_HEADS = 4
HEAD_SIZE = 128
CONTEXT_LENGTH = 256
GROUP = QUERY_HEADS // KEY_VALUE_HEADS
QUERY_WIDTH = QUERY_HEADS * HEAD_SIZE
QKVW = QUERY_WIDTH + 2 * KEY_VALUE_HEADS * HEAD_SIZE
TILE = 1024
COLUMNS = 256
ORDERS = ("is", "is")
LANES = 128
MIB = 1024 * 1024
CHUNKS = ((2, 4), (0, 2))


def stage_bits(count, phase):
    bits = []
    bit = 2
    while bit < count:
        bits.append(bit)
        bit *= 2
    swapped = bits[1:2] + bits[:1] + bits[2:]
    rotated = bits[1:] + bits[:1]
    return [{"i": bits, "s": swapped, "r": rotated, "z": bits[:1] + bits[2:] + bits[1:2]}[name] for name in ORDERS[phase]]


def parity(index, count):
    result, shift = index, 1
    while 1 << shift < count:
        result = result ^ (index >> shift)
        shift += 1
    return result & 1


def place(index, count, phase, order):
    result, size = 0, count // 2
    for bit in stage_bits(count, phase)[order]:
        size //= 2
        result = result | ((index >> (bit.bit_length() - 1)) & 1) * size
    return result


def places(me, count, phase):
    own = [place(me, count, phase, order) for order in range(2)]
    result = []
    for block in range(count):
        order = parity(block, count)
        half = jnp.bitwise_xor(parity(me, count), order) * (count // 2)
        result.append(half + jnp.bitwise_xor(own[order], place(block, count, phase, order)))
    return result


def fetch(w_ref, weights, sems, start, tiles):
    copies = [
        pltpu.make_async_copy(
            w_ref.at[:, pl.ds(start + tile * TILE, TILE)], weights.at[tile], sems.at[tile]
        )
        for tile in range(tiles)
    ]
    return copies


def multiply(copies, scaled, weights, send_ref, keep_ref):
    half = keep_ref.shape[0]
    for tile in range(weights.shape[0]):
        if copies:
            copies[tile].wait()
        product = jnp.dot(scaled[...], weights[tile], preferred_element_type=jnp.float32)
        columns = slice(tile * TILE, (tile + 1) * TILE)
        keep_ref[:, columns] = product[:half]
        send_ref[:, columns] = product[half:].astype(jnp.bfloat16)


def first_kernel(
    count, rows, span, later_span,
    me_ref, acts_ref, gain_ref, w_ref, send_ref, keep_ref, scaled, later_weights,
    narrow, gains, ordered, squares, weights, small_sems, sems, later_sems,
):
    start, width = span
    half = count * rows // 2
    me = me_ref[0]
    small = [
        pltpu.make_async_copy(acts_ref, narrow, small_sems.at[0]),
        pltpu.make_async_copy(gain_ref, gains, small_sems.at[1]),
    ]
    copies = fetch(w_ref, weights, sems, start, width // TILE)
    later = fetch(w_ref, later_weights, later_sems, later_span[0], later_span[1] // TILE)
    for copy in small + copies + later:
        copy.start()
    for copy in small:
        copy.wait()
    gain = gains[...].astype(jnp.float32)[None, :]
    lane = lax.broadcasted_iota(jnp.int32, (rows, LANES), 1)
    targets = places(me, count, 0)
    for pair in range(count // 2):
        both = narrow[2 * pair * rows : 2 * (pair + 1) * rows, :].astype(jnp.float32)
        for side in range(2):
            wide = both[side * rows : (side + 1) * rows]
            target = targets[2 * pair + side]
            where = pl.ds(pl.multiple_of(target * rows, rows), rows)
            ordered[where, :] = wide * gain
            total = jnp.sum(wide * wide, axis=1, keepdims=True)
            high = total.astype(jnp.bfloat16).astype(jnp.float32)
            lanes = jnp.where(lane == 2 * me, high, 0.0)
            squares[where, :] = jnp.where(lane == 2 * me + 1, total - high, lanes)
    scaled[...] = ordered[...].astype(jnp.bfloat16)
    keep_ref[:, width:] = squares[:half]
    send_ref[:, width:] = squares[half:].astype(jnp.bfloat16)
    multiply(copies, scaled, weights, send_ref, keep_ref)
    for copy in later:
        copy.wait()


def later_kernel(scaled, weights, send_ref, keep_ref):
    multiply(None, scaled, weights, send_ref, keep_ref)


def project(me, activations, gain, w_qkv, count, rows, spans):
    depth = w_qkv.shape[0]
    half = count * rows // 2
    in_hbm = pl.BlockSpec(memory_space=pltpu.HBM)
    in_vmem = pl.BlockSpec(memory_space=pltpu.VMEM)

    def call(kernel, in_specs, operands, width, whole, more_out, scratch):
        out_shape = [
            jax.ShapeDtypeStruct((half, whole), jnp.bfloat16),
            jax.ShapeDtypeStruct((half, whole), jnp.float32),
        ] + more_out
        return pl.pallas_call(
            kernel,
            in_specs=in_specs,
            out_specs=[in_vmem] * len(out_shape),
            scratch_shapes=scratch,
            out_shape=out_shape,
            compiler_params=pltpu.CompilerParams(vmem_limit_bytes=28 * MIB),
            cost_estimate=pl.CostEstimate(
                flops=4 * half * depth * width,
                bytes_accessed=2 * depth * width + 6 * half * whole,
                transcendentals=0,
            ),
        )(*operands)

    tiles, later_tiles = [width // TILE for _, width in spans]
    width, later_width = [width for _, width in spans]
    send, keep, scaled, weights = call(
        functools.partial(first_kernel, count, rows, *spans),
        [pl.BlockSpec(memory_space=pltpu.SMEM)] + [in_hbm] * 3,
        (me, activations, gain, w_qkv),
        width,
        width + LANES,
        [
            jax.ShapeDtypeStruct(activations.shape, jnp.bfloat16),
            jax.ShapeDtypeStruct((later_tiles, depth, TILE), jnp.bfloat16),
        ],
        [
            pltpu.VMEM(activations.shape, jnp.bfloat16),
            pltpu.VMEM(gain.shape, jnp.bfloat16),
            pltpu.VMEM(activations.shape, jnp.float32),
            pltpu.VMEM((2 * half, LANES), jnp.float32),
            pltpu.VMEM((tiles, depth, TILE), jnp.bfloat16),
            pltpu.SemaphoreType.DMA((2,)),
            pltpu.SemaphoreType.DMA((tiles,)),
            pltpu.SemaphoreType.DMA((later_tiles,)),
        ],
    )
    later = call(
        later_kernel, [in_vmem] * 2, (scaled, weights), later_width, later_width, [], []
    )
    return (send, keep), later


def output_kernel(count, rows, start, me_ref, mine_ref, other_ref, w_ref, *refs):
    *before, out_ref, total = refs
    depth = mine_ref.shape[1]
    left = jnp.concatenate([mine_ref[...], other_ref[...]], axis=0)
    last = out_ref.dtype != jnp.float32
    width = min(COLUMNS, total.shape[1])
    for column in range(0, total.shape[1], width):
        columns = slice(column, column + width)
        product = jnp.dot(
            left, w_ref[start : start + depth, columns], preferred_element_type=jnp.float32
        )
        for part in before:
            product += part[:, columns]
        if last:
            total[:, columns] = product
        else:
            out_ref[:, columns] = product
    if not last:
        return
    sources = places(me_ref[0], count, 1)
    for pair in range(count // 2):
        parts = []
        for source in sources[2 * pair : 2 * pair + 2]:
            parts.append(total[pl.ds(pl.multiple_of(source * rows, rows), rows), :])
        where = slice(2 * pair * rows, 2 * (pair + 1) * rows)
        out_ref[where, :] = jnp.concatenate(parts, axis=0).astype(out_ref.dtype)


def output_part(me, mine, other, w_out, before, count, rows, start, last):
    depth, columns = mine.shape[1], w_out.shape[1]
    shape = (count * rows, columns)
    operands = (mine, other, w_out) + (() if before is None else (before,))
    in_vmem = pl.BlockSpec(memory_space=pltpu.VMEM)
    return pl.pallas_call(
        functools.partial(output_kernel, count, rows, start),
        in_specs=[pl.BlockSpec(memory_space=pltpu.SMEM)] + [in_vmem] * len(operands),
        out_specs=in_vmem,
        scratch_shapes=[pltpu.VMEM(shape, jnp.float32)],
        out_shape=jax.ShapeDtypeStruct(shape, jnp.bfloat16 if last else jnp.float32),
        compiler_params=pltpu.CompilerParams(vmem_limit_bytes=28 * MIB),
        cost_estimate=pl.CostEstimate(
            flops=2 * shape[0] * depth * columns,
            bytes_accessed=2 * depth * columns + 2 * shape[0] * (depth + columns),
            transcendentals=0,
        ),
    )(me, *operands)


def rotation():
    half_dim = HEAD_SIZE // 2
    frequency = jnp.float32(500000.0) ** (
        -jnp.arange(half_dim, dtype=jnp.float32) * 2.0 / HEAD_SIZE
    )
    angles = jnp.float32(CONTEXT_LENGTH) * frequency
    return jnp.cos(angles), jnp.sin(angles)


def apply_rotary(tensor):
    half_dim = HEAD_SIZE // 2
    cosine, sine_part = rotation()
    first_half = tensor[..., :half_dim]
    second_half = tensor[..., half_dim:]
    return jnp.concatenate(
        [
            first_half * cosine - second_half * sine_part,
            second_half * cosine + first_half * sine_part,
        ],
        axis=-1,
    )


def attend(query_rows, fresh_keys, fresh_values, cache_keys, value_cache_rows):
    count_of_rows, heads = fresh_keys.shape[:2]
    grouped_queries = query_rows.reshape(count_of_rows, heads, GROUP, HEAD_SIZE)
    scaling = 1.0 / jnp.sqrt(jnp.float32(HEAD_SIZE))
    cached_scores = (
        jnp.einsum(
            "rkgd,rtkd->rkgt", grouped_queries, cache_keys, preferred_element_type=jnp.float32
        )
        * scaling
    )
    own_scores = (
        jnp.einsum("rkgd,rkd->rkg", grouped_queries, fresh_keys, preferred_element_type=jnp.float32)
        * scaling
    )
    highest = jnp.maximum(jnp.max(cached_scores, axis=-1), own_scores)
    cached_exp = jnp.exp(cached_scores - highest[..., None])
    own_exp = jnp.exp(own_scores - highest)
    denominator = jnp.sum(cached_exp, axis=-1) + own_exp
    cached_weights = (cached_exp / denominator[..., None]).astype(jnp.bfloat16)
    own_weights = (own_exp / denominator).astype(jnp.bfloat16)
    combined = jnp.einsum(
        "rkgt,rtkd->rkgd", cached_weights, value_cache_rows, preferred_element_type=jnp.float32
    )
    combined = (
        combined
        + own_weights.astype(jnp.float32)[..., None]
        * fresh_values.astype(jnp.float32)[:, :, None, :]
    )
    return combined.reshape(count_of_rows, heads * GROUP * HEAD_SIZE).astype(jnp.bfloat16)


def swap(value, count, phase=None, stage=None):
    orders = None if phase is None else stage_bits(count, phase)
    partners = []
    for i in range(count):
        mask = 1 if phase is None else orders[parity(i, count)][stage] ^ 1
        partners.append((i, i ^ mask))
    return lax.ppermute(value, "gx", partners)


def tie(value, token):
    return lax.optimization_barrier((value, token))[0]


class Reduction:
    def __init__(self, send, keep, count, rows):
        self.keep, self.count, self.rows = keep, count, rows
        self.size = count // 2
        self.received = [swap(send, count)]

    def combine(self, part):
        total = self.keep[part]
        for piece in self.received:
            total = total + piece[part].astype(jnp.float32)
        return total

    def stage(self):
        self.size //= 2
        part = slice(self.size * self.rows, 2 * self.size * self.rows)
        send = self.combine(part).astype(jnp.bfloat16)
        self.received.append(swap(send, self.count, 0, len(self.received) - 1))
        return send

    def own(self):
        return self.combine(slice(0, self.rows))


def body(count, activations, norm_gain, w_qkv, w_out, cache_keys, value_cache_rows):
    rows = cache_keys.shape[0]
    me = lax.axis_index("gx").astype(jnp.int32)[None]
    activations, norm_gain, w_qkv = [
        pltpu.with_memory_space_constraint(value, pltpu.HBM)
        for value in (activations, norm_gain, w_qkv)
    ]
    per_head = GROUP * HEAD_SIZE

    spans = []
    for order, (low, high) in enumerate(CHUNKS):
        start = low * per_head
        spans.append((start, (high * per_head if order else QKVW) - start))
    parts = []
    for send, keep in project(me, activations, norm_gain, w_qkv, count, rows, spans):
        parts.append(Reduction(send, keep, count, rows))
    w_out = tie(w_out, send)
    stages = len(stage_bits(count, 0)[0])
    for stage in range(stages):
        for part in parts:
            token = part.stage()
        if stage == 0:
            cache_keys = tie(cache_keys, token)
            value_cache_rows = tie(value_cache_rows, token)
    gathered = []
    for order, (low, high) in enumerate(CHUNKS):
        width = (high - low) * per_head
        if order > 0:
            parts[order].keep = tie(parts[order].keep, gathered[-1])
        sums = parts[order].own()
        if order == 0:
            own_squares = jnp.sum(sums[:, -LANES:], axis=1)
            inverse_rms = lax.rsqrt(own_squares / D + 1e-05)[:, None]
            fresh = sums[:, width:-LANES] * inverse_rms
            kv_width = KEY_VALUE_HEADS * HEAD_SIZE
            shape = (rows, KEY_VALUE_HEADS, HEAD_SIZE)
            fresh_keys = apply_rotary(fresh[:, :kv_width].reshape(shape)).astype(jnp.bfloat16)
            fresh_values = fresh[:, kv_width:].reshape(shape).astype(jnp.bfloat16)
        queries = apply_rotary(
            (sums[:, :width] * inverse_rms).reshape(rows, width // HEAD_SIZE, HEAD_SIZE)
        ).astype(jnp.bfloat16)
        gathered.append(
            attend(
                queries,
                fresh_keys[:, low:high],
                fresh_values[:, low:high],
                cache_keys[:, :, low:high],
                value_cache_rows[:, :, low:high],
            )
        )

    for stage in reversed(range(stages)):
        before = None
        for order in range(len(CHUNKS)):
            mine = gathered[order]
            if before is not None:
                mine = tie(mine, before)
            before = mine
            gathered[order] = jnp.concatenate([mine, swap(mine, count, 1, stage)], axis=0)
    total = None
    for order, (low, high) in enumerate(CHUNKS):
        mine = gathered[order]
        other = swap(mine, count)
        total = output_part(
            me, mine, other, w_out, total, count, rows, low * per_head,
            order == len(CHUNKS) - 1,
        )
    return total


def solution(mesh):
    return jax.shard_map(
        functools.partial(body, mesh.shape["gx"]),
        mesh=mesh,
        in_specs=(
            P("groups", "gx"),
            P("gx"),
            P("gx", None),
            P(None, "gx"),
            P(("groups", "gx"), None, None, None),
            P(("groups", "gx"), None, None, None),
        ),
        out_specs=P("groups", "gx"),
        check_vma=False,
    )
```

```python
import functools

import jax
import jax.numpy as jnp
from jax import lax
from jax.experimental import pallas as pl
from jax.experimental.pallas import tpu as pltpu
from jax.sharding import PartitionSpec as P

D = 16384
QUERY_HEADS = 64
KEY_VALUE_HEADS = 4
HEAD_SIZE = 128
CONTEXT_LENGTH = 256
GROUP = QUERY_HEADS // KEY_VALUE_HEADS
QUERY_WIDTH = QUERY_HEADS * HEAD_SIZE
QKVW = QUERY_WIDTH + 2 * KEY_VALUE_HEADS * HEAD_SIZE
TILE = 1024
COLUMNS = 256
LANES = 128
MIB = 1024 * 1024
CHUNKS = ((2, 4), (0, 2))
ORDERS = ("ir", "is", "si")
GATHER = len(CHUNKS)


def stage_bits(count, phase):
    bits = []
    bit = 2
    while bit < count:
        bits.append(bit)
        bit *= 2
    swapped = bits[1:2] + bits[:1] + bits[2:]
    rotated = bits[1:] + bits[:1]
    return [{"i": bits, "s": swapped, "r": rotated, "z": bits[:1] + bits[2:] + bits[1:2]}[name] for name in ORDERS[phase]]


def parity(index, count):
    result, shift = index, 1
    while 1 << shift < count:
        result = result ^ (index >> shift)
        shift += 1
    return result & 1


def place(index, count, phase, order):
    result, size = 0, count // 2
    for bit in stage_bits(count, phase)[order]:
        size //= 2
        result = result | ((index >> (bit.bit_length() - 1)) & 1) * size
    return result


def places(me, count, phase):
    own = [place(me, count, phase, order) for order in range(2)]
    result = []
    my_order = parity(me, count)
    for block in range(count):
        order = parity(block, count)
        half = jnp.bitwise_xor(my_order, order) * (count // 2)
        result.append(half + jnp.bitwise_xor(own[order], place(block, count, phase, order)))
    return result


def fetch(w_ref, weights, sems, start, tiles):
    copies = [
        pltpu.make_async_copy(
            w_ref.at[:, pl.ds(start + tile * TILE, TILE)], weights.at[tile], sems.at[tile]
        )
        for tile in range(tiles)
    ]
    return copies


def multiply(copies, scaled, weights, send_ref, keep_ref):
    half = keep_ref.shape[0]
    for tile in range(weights.shape[0]):
        if copies:
            copies[tile].wait()
        product = jnp.dot(scaled[...], weights[tile], preferred_element_type=jnp.float32)
        columns = slice(tile * TILE, (tile + 1) * TILE)
        keep_ref[:, columns] = product[:half]
        send_ref[:, columns] = product[half:].astype(jnp.bfloat16)


def first_kernel(
    count, rows, span, later_span,
    me_ref, acts_ref, gain_ref, w_ref, send_ref, keep_ref, later_scaled, later_weights,
    narrow, gains, ordered, scaled, squares, weights, small_sems, sems, later_sems,
):
    start, width = span
    half = count * rows // 2
    me = me_ref[0]
    small = [
        pltpu.make_async_copy(acts_ref, narrow, small_sems.at[0]),
        pltpu.make_async_copy(gain_ref, gains, small_sems.at[1]),
    ]
    copies = fetch(w_ref, weights, sems, start, width // TILE)
    later = fetch(w_ref, later_weights, later_sems, later_span[0], later_span[1] // TILE)
    for copy in small + copies + later:
        copy.start()
    for copy in small:
        copy.wait()
    gain = gains[...].astype(jnp.float32)[None, :]
    lane = lax.broadcasted_iota(jnp.int32, (rows, LANES), 1)
    for chunk, target_ref in ((1, later_scaled), (0, scaled)):
        targets = places(me, count, chunk)
        for pair in range(count // 2):
            both = narrow[2 * pair * rows : 2 * (pair + 1) * rows, :].astype(jnp.float32)
            for side in range(2):
                wide = both[side * rows : (side + 1) * rows]
                target = targets[2 * pair + side]
                where = pl.ds(pl.multiple_of(target * rows, rows), rows)
                ordered[where, :] = wide * gain
                if chunk > 0:
                    continue
                total = jnp.sum(wide * wide, axis=1, keepdims=True)
                high = total.astype(jnp.bfloat16).astype(jnp.float32)
                lanes = jnp.where(lane == 2 * me, high, 0.0)
                squares[where, :] = jnp.where(lane == 2 * me + 1, total - high, lanes)
        target_ref[...] = ordered[...].astype(jnp.bfloat16)
    keep_ref[:, width:] = squares[:half]
    send_ref[:, width:] = squares[half:].astype(jnp.bfloat16)
    multiply(copies, scaled, weights, send_ref, keep_ref)
    for copy in later:
        copy.wait()


def later_kernel(scaled, weights, send_ref, keep_ref):
    multiply(None, scaled, weights, send_ref, keep_ref)


def project(me, activations, gain, w_qkv, count, rows, spans):
    depth = w_qkv.shape[0]
    half = count * rows // 2
    in_hbm = pl.BlockSpec(memory_space=pltpu.HBM)
    in_vmem = pl.BlockSpec(memory_space=pltpu.VMEM)

    def call(kernel, in_specs, operands, width, whole, more_out, scratch):
        out_shape = [
            jax.ShapeDtypeStruct((half, whole), jnp.bfloat16),
            jax.ShapeDtypeStruct((half, whole), jnp.float32),
        ] + more_out
        return pl.pallas_call(
            kernel,
            in_specs=in_specs,
            out_specs=[in_vmem] * len(out_shape),
            scratch_shapes=scratch,
            out_shape=out_shape,
            compiler_params=pltpu.CompilerParams(vmem_limit_bytes=28 * MIB),
            cost_estimate=pl.CostEstimate(
                flops=4 * half * depth * width,
                bytes_accessed=2 * depth * width + 6 * half * whole,
                transcendentals=0,
            ),
        )(*operands)

    tiles, later_tiles = [width // TILE for _, width in spans]
    width, later_width = [width for _, width in spans]
    send, keep, scaled, weights = call(
        functools.partial(first_kernel, count, rows, *spans),
        [pl.BlockSpec(memory_space=pltpu.SMEM)] + [in_hbm] * 3,
        (me, activations, gain, w_qkv),
        width,
        width + LANES,
        [
            jax.ShapeDtypeStruct(activations.shape, jnp.bfloat16),
            jax.ShapeDtypeStruct((later_tiles, depth, TILE), jnp.bfloat16),
        ],
        [
            pltpu.VMEM(activations.shape, jnp.bfloat16),
            pltpu.VMEM(gain.shape, jnp.bfloat16),
            pltpu.VMEM(activations.shape, jnp.float32),
            pltpu.VMEM(activations.shape, jnp.bfloat16),
            pltpu.VMEM((2 * half, LANES), jnp.float32),
            pltpu.VMEM((tiles, depth, TILE), jnp.bfloat16),
            pltpu.SemaphoreType.DMA((2,)),
            pltpu.SemaphoreType.DMA((tiles,)),
            pltpu.SemaphoreType.DMA((later_tiles,)),
        ],
    )
    later = call(
        later_kernel, [in_vmem] * 2, (scaled, weights), later_width, later_width, [], []
    )
    return (send, keep), later


def output_kernel(count, rows, start, me_ref, mine_ref, other_ref, w_ref, *refs):
    *before, out_ref, total = refs
    depth = mine_ref.shape[1]
    left = jnp.concatenate([mine_ref[...], other_ref[...]], axis=0)
    last = out_ref.dtype != jnp.float32
    width = min(COLUMNS, total.shape[1])
    for column in range(0, total.shape[1], width):
        columns = slice(column, column + width)
        product = jnp.dot(
            left, w_ref[start : start + depth, columns], preferred_element_type=jnp.float32
        )
        for part in before:
            product += part[:, columns]
        if last:
            total[:, columns] = product
        else:
            out_ref[:, columns] = product
    if not last:
        return
    sources = places(me_ref[0], count, GATHER)
    for pair in range(count // 2):
        parts = []
        for source in sources[2 * pair : 2 * pair + 2]:
            parts.append(total[pl.ds(pl.multiple_of(source * rows, rows), rows), :])
        where = slice(2 * pair * rows, 2 * (pair + 1) * rows)
        out_ref[where, :] = jnp.concatenate(parts, axis=0).astype(out_ref.dtype)


def output_part(me, mine, other, w_out, before, count, rows, start, last):
    depth, columns = mine.shape[1], w_out.shape[1]
    shape = (count * rows, columns)
    operands = (mine, other, w_out) + (() if before is None else (before,))
    in_vmem = pl.BlockSpec(memory_space=pltpu.VMEM)
    return pl.pallas_call(
        functools.partial(output_kernel, count, rows, start),
        in_specs=[pl.BlockSpec(memory_space=pltpu.SMEM)] + [in_vmem] * len(operands),
        out_specs=in_vmem,
        scratch_shapes=[pltpu.VMEM(shape, jnp.float32)],
        out_shape=jax.ShapeDtypeStruct(shape, jnp.bfloat16 if last else jnp.float32),
        compiler_params=pltpu.CompilerParams(vmem_limit_bytes=28 * MIB),
        cost_estimate=pl.CostEstimate(
            flops=2 * shape[0] * depth * columns,
            bytes_accessed=2 * depth * columns + 2 * shape[0] * (depth + columns),
            transcendentals=0,
        ),
    )(me, *operands)


def rotation():
    half_dim = HEAD_SIZE // 2
    frequency = jnp.float32(500000.0) ** (
        -jnp.arange(half_dim, dtype=jnp.float32) * 2.0 / HEAD_SIZE
    )
    angles = jnp.float32(CONTEXT_LENGTH) * frequency
    return jnp.cos(angles), jnp.sin(angles)


def apply_rotary(tensor):
    half_dim = HEAD_SIZE // 2
    cosine, sine_part = rotation()
    first_half = tensor[..., :half_dim]
    second_half = tensor[..., half_dim:]
    return jnp.concatenate(
        [
            first_half * cosine - second_half * sine_part,
            second_half * cosine + first_half * sine_part,
        ],
        axis=-1,
    )


def attend(query_rows, fresh_keys, fresh_values, cache_keys, value_cache_rows):
    count_of_rows, heads = fresh_keys.shape[:2]
    grouped_queries = query_rows.reshape(count_of_rows, heads, GROUP, HEAD_SIZE)
    scaling = 1.0 / jnp.sqrt(jnp.float32(HEAD_SIZE))
    cached_scores = (
        jnp.einsum(
            "rkgd,rtkd->rkgt", grouped_queries, cache_keys, preferred_element_type=jnp.float32
        )
        * scaling
    )
    own_scores = (
        jnp.einsum("rkgd,rkd->rkg", grouped_queries, fresh_keys, preferred_element_type=jnp.float32)
        * scaling
    )
    highest = jnp.maximum(jnp.max(cached_scores, axis=-1), own_scores)
    cached_exp = jnp.exp(cached_scores - highest[..., None])
    own_exp = jnp.exp(own_scores - highest)
    denominator = jnp.sum(cached_exp, axis=-1) + own_exp
    cached_weights = (cached_exp / denominator[..., None]).astype(jnp.bfloat16)
    own_weights = (own_exp / denominator).astype(jnp.bfloat16)
    combined = jnp.einsum(
        "rkgt,rtkd->rkgd", cached_weights, value_cache_rows, preferred_element_type=jnp.float32
    )
    combined = (
        combined
        + own_weights.astype(jnp.float32)[..., None]
        * fresh_values.astype(jnp.float32)[:, :, None, :]
    )
    return combined.reshape(count_of_rows, heads * GROUP * HEAD_SIZE).astype(jnp.bfloat16)


def swap(value, count, phase=None, stage=None):
    orders = None if phase is None else stage_bits(count, phase)
    partners = []
    for i in range(count):
        mask = 1 if phase is None else orders[parity(i, count)][stage] ^ 1
        partners.append((i, i ^ mask))
    return lax.ppermute(value, "gx", partners)


def tie(value, token):
    return lax.optimization_barrier((value, token))[0]


class Reduction:
    def __init__(self, send, keep, count, rows, chunk):
        self.chunk = chunk
        self.keep, self.count, self.rows = keep, count, rows
        self.size = count // 2
        self.received = [swap(send, count)]

    def combine(self, part):
        total = self.keep[part]
        for piece in self.received:
            total = total + piece[part].astype(jnp.float32)
        return total

    def stage(self):
        self.size //= 2
        part = slice(self.size * self.rows, 2 * self.size * self.rows)
        send = self.combine(part).astype(jnp.bfloat16)
        self.received.append(swap(send, self.count, self.chunk, len(self.received) - 1))
        return send

    def own(self):
        return self.combine(slice(0, self.rows))


def body(count, activations, norm_gain, w_qkv, w_out, cache_keys, value_cache_rows):
    rows = cache_keys.shape[0]
    me = lax.axis_index("gx").astype(jnp.int32)[None]
    activations, norm_gain, w_qkv = [
        pltpu.with_memory_space_constraint(value, pltpu.HBM)
        for value in (activations, norm_gain, w_qkv)
    ]
    per_head = GROUP * HEAD_SIZE

    spans = []
    for order, (low, high) in enumerate(CHUNKS):
        start = low * per_head
        spans.append((start, (high * per_head if order else QKVW) - start))
    parts = []
    for send, keep in project(me, activations, norm_gain, w_qkv, count, rows, spans):
        parts.append(Reduction(send, keep, count, rows, len(parts)))
    w_out = tie(w_out, send)
    stages = len(stage_bits(count, 0)[0])
    for stage in range(stages):
        for part in parts:
            token = part.stage()
        if stage == 0:
            cache_keys = tie(cache_keys, token)
            value_cache_rows = tie(value_cache_rows, token)
    gathered = []
    for order, (low, high) in enumerate(CHUNKS):
        width = (high - low) * per_head
        if order > 0:
            parts[order].keep = tie(parts[order].keep, gathered[-1])
        sums = parts[order].own()
        if order == 0:
            own_squares = jnp.sum(sums[:, -LANES:], axis=1)
            inverse_rms = lax.rsqrt(own_squares / D + 1e-05)[:, None]
            fresh = sums[:, width:-LANES] * inverse_rms
            kv_width = KEY_VALUE_HEADS * HEAD_SIZE
            shape = (rows, KEY_VALUE_HEADS, HEAD_SIZE)
            fresh_keys = apply_rotary(fresh[:, :kv_width].reshape(shape)).astype(jnp.bfloat16)
            fresh_values = fresh[:, kv_width:].reshape(shape).astype(jnp.bfloat16)
        queries = apply_rotary(
            (sums[:, :width] * inverse_rms).reshape(rows, width // HEAD_SIZE, HEAD_SIZE)
        ).astype(jnp.bfloat16)
        gathered.append(
            attend(
                queries,
                fresh_keys[:, low:high],
                fresh_values[:, low:high],
                cache_keys[:, :, low:high],
                value_cache_rows[:, :, low:high],
            )
        )

    for stage in reversed(range(stages)):
        before = None
        for order in range(len(CHUNKS)):
            mine = gathered[order]
            if before is not None:
                mine = tie(mine, before)
            before = mine
            gathered[order] = jnp.concatenate([mine, swap(mine, count, GATHER, stage)], axis=0)
    total = None
    for order, (low, high) in enumerate(CHUNKS):
        mine = gathered[order]
        other = swap(mine, count)
        total = output_part(
            me, mine, other, w_out, total, count, rows, low * per_head,
            order == len(CHUNKS) - 1,
        )
    return total


def solution(mesh):
    return jax.shard_map(
        functools.partial(body, mesh.shape["gx"]),
        mesh=mesh,
        in_specs=(
            P("groups", "gx"),
            P("gx"),
            P("gx", None),
            P(None, "gx"),
            P(("groups", "gx"), None, None, None),
            P(("groups", "gx"), None, None, None),
        ),
        out_specs=P("groups", "gx"),
        check_vma=False,
    )
```

```python
import functools

import jax
import jax.numpy as jnp
from jax import lax
from jax.experimental import pallas as pl
from jax.experimental.pallas import tpu as pltpu
from jax.sharding import PartitionSpec as P

D = 16384
QUERY_HEADS = 64
KEY_VALUE_HEADS = 4
HEAD_SIZE = 128
CONTEXT_LENGTH = 256
GROUP = QUERY_HEADS // KEY_VALUE_HEADS
QUERY_WIDTH = QUERY_HEADS * HEAD_SIZE
QKVW = QUERY_WIDTH + 2 * KEY_VALUE_HEADS * HEAD_SIZE
TILE = 1024
COLUMNS = 256
LANES = 128
MIB = 1024 * 1024
CHUNKS = ((2, 4), (0, 2))
ORDERS = ("ir", "is", "si")
GATHER = len(CHUNKS)


def stage_bits(count, phase):
    bits = []
    bit = 2
    while bit < count:
        bits.append(bit)
        bit *= 2
    swapped = bits[1:2] + bits[:1] + bits[2:]
    rotated = bits[1:] + bits[:1]
    return [{"i": bits, "s": swapped, "r": rotated, "z": bits[:1] + bits[2:] + bits[1:2]}[name] for name in ORDERS[phase]]


def parity(index, count):
    result, shift = index, 1
    while 1 << shift < count:
        result = result ^ (index >> shift)
        shift += 1
    return result & 1


def place(index, count, phase, order):
    result, size = 0, count // 2
    for bit in stage_bits(count, phase)[order]:
        size //= 2
        result = result | ((index >> (bit.bit_length() - 1)) & 1) * size
    return result


def places(me, count, phase):
    own = [place(me, count, phase, order) for order in range(2)]
    result = []
    my_order = parity(me, count)
    for block in range(count):
        order = parity(block, count)
        half = jnp.bitwise_xor(my_order, order) * (count // 2)
        result.append(half + jnp.bitwise_xor(own[order], place(block, count, phase, order)))
    return result


def fetch(w_ref, weights, sems, start, tiles):
    copies = [
        pltpu.make_async_copy(
            w_ref.at[:, pl.ds(start + tile * TILE, TILE)], weights.at[tile], sems.at[tile]
        )
        for tile in range(tiles)
    ]
    return copies


def multiply(copies, scaled, weights, send_ref, keep_ref):
    half = keep_ref.shape[0]
    for tile in range(weights.shape[0]):
        if copies:
            copies[tile].wait()
        product = jnp.dot(scaled[...], weights[tile], preferred_element_type=jnp.float32)
        columns = slice(tile * TILE, (tile + 1) * TILE)
        keep_ref[:, columns] = product[:half]
        send_ref[:, columns] = product[half:].astype(jnp.bfloat16)


def first_kernel(
    count, rows, span, later_span,
    me_ref, acts_ref, gain_ref, w_ref, send_ref, keep_ref, later_scaled, later_weights,
    narrow, gains, ordered, scaled, squares, weights, small_sems, sems, later_sems,
):
    start, width = span
    half = count * rows // 2
    me = me_ref[0]
    small = [
        pltpu.make_async_copy(acts_ref, narrow, small_sems.at[0]),
        pltpu.make_async_copy(gain_ref, gains, small_sems.at[1]),
    ]
    copies = fetch(w_ref, weights, sems, start, width // TILE)
    later = fetch(w_ref, later_weights, later_sems, later_span[0], later_span[1] // TILE)
    for copy in small + copies + later:
        copy.start()
    for copy in small:
        copy.wait()
    gain = gains[...].astype(jnp.float32)[None, :]
    lane = lax.broadcasted_iota(jnp.int32, (rows, LANES), 1)
    for chunk, target_ref in ((1, later_scaled), (0, scaled)):
        targets = places(me, count, chunk)
        for pair in range(count // 2):
            both = narrow[2 * pair * rows : 2 * (pair + 1) * rows, :].astype(jnp.float32)
            for side in range(2):
                wide = both[side * rows : (side + 1) * rows]
                target = targets[2 * pair + side]
                where = pl.ds(pl.multiple_of(target * rows, rows), rows)
                ordered[where, :] = wide * gain
                if chunk > 0:
                    continue
                total = jnp.sum(wide * wide, axis=1, keepdims=True)
                high = total.astype(jnp.bfloat16).astype(jnp.float32)
                lanes = jnp.where(lane == 2 * me, high, 0.0)
                squares[where, :] = jnp.where(lane == 2 * me + 1, total - high, lanes)
        target_ref[...] = ordered[...].astype(jnp.bfloat16)
    keep_ref[:, width:] = squares[:half]
    send_ref[:, width:] = squares[half:].astype(jnp.bfloat16)
    multiply(copies, scaled, weights, send_ref, keep_ref)
    for copy in later:
        copy.wait()


def later_kernel(scaled, weights, send_ref, keep_ref):
    multiply(None, scaled, weights, send_ref, keep_ref)


def project(me, activations, gain, w_qkv, count, rows, spans):
    depth = w_qkv.shape[0]
    half = count * rows // 2
    in_hbm = pl.BlockSpec(memory_space=pltpu.HBM)
    in_vmem = pl.BlockSpec(memory_space=pltpu.VMEM)

    def call(kernel, in_specs, operands, width, whole, more_out, scratch):
        out_shape = [
            jax.ShapeDtypeStruct((half, whole), jnp.bfloat16),
            jax.ShapeDtypeStruct((half, whole), jnp.float32),
        ] + more_out
        return pl.pallas_call(
            kernel,
            in_specs=in_specs,
            out_specs=[in_vmem] * len(out_shape),
            scratch_shapes=scratch,
            out_shape=out_shape,
            compiler_params=pltpu.CompilerParams(vmem_limit_bytes=28 * MIB),
            cost_estimate=pl.CostEstimate(
                flops=4 * half * depth * width,
                bytes_accessed=2 * depth * width + 6 * half * whole,
                transcendentals=0,
            ),
        )(*operands)

    tiles, later_tiles = [width // TILE for _, width in spans]
    width, later_width = [width for _, width in spans]
    send, keep, scaled, weights = call(
        functools.partial(first_kernel, count, rows, *spans),
        [pl.BlockSpec(memory_space=pltpu.SMEM)] + [in_hbm] * 3,
        (me, activations, gain, w_qkv),
        width,
        width + LANES,
        [
            jax.ShapeDtypeStruct(activations.shape, jnp.bfloat16),
            jax.ShapeDtypeStruct((later_tiles, depth, TILE), jnp.bfloat16),
        ],
        [
            pltpu.VMEM(activations.shape, jnp.bfloat16),
            pltpu.VMEM(gain.shape, jnp.bfloat16),
            pltpu.VMEM(activations.shape, jnp.float32),
            pltpu.VMEM(activations.shape, jnp.bfloat16),
            pltpu.VMEM((2 * half, LANES), jnp.float32),
            pltpu.VMEM((tiles, depth, TILE), jnp.bfloat16),
            pltpu.SemaphoreType.DMA((2,)),
            pltpu.SemaphoreType.DMA((tiles,)),
            pltpu.SemaphoreType.DMA((later_tiles,)),
        ],
    )
    later = call(
        later_kernel, [in_vmem] * 2, (scaled, weights), later_width, later_width, [], []
    )
    return (send, keep), later


def output_kernel(count, rows, start, me_ref, mine_ref, other_ref, w_ref, *refs):
    *before, out_ref, total = refs
    depth = mine_ref.shape[1]
    left = jnp.concatenate([mine_ref[...], other_ref[...]], axis=0)
    last = out_ref.dtype != jnp.float32
    width = min(COLUMNS, total.shape[1])
    for column in range(0, total.shape[1], width):
        columns = slice(column, column + width)
        product = jnp.dot(
            left, w_ref[start : start + depth, columns], preferred_element_type=jnp.float32
        )
        for part in before:
            product += part[:, columns]
        if last:
            total[:, columns] = product
        else:
            out_ref[:, columns] = product
    if not last:
        return
    sources = places(me_ref[0], count, GATHER)
    for pair in range(count // 2):
        parts = []
        for source in sources[2 * pair : 2 * pair + 2]:
            parts.append(total[pl.ds(pl.multiple_of(source * rows, rows), rows), :])
        where = slice(2 * pair * rows, 2 * (pair + 1) * rows)
        out_ref[where, :] = jnp.concatenate(parts, axis=0).astype(out_ref.dtype)


def output_part(me, mine, other, w_out, before, count, rows, start, last):
    depth, columns = mine.shape[1], w_out.shape[1]
    shape = (count * rows, columns)
    operands = (mine, other, w_out) + (() if before is None else (before,))
    in_vmem = pl.BlockSpec(memory_space=pltpu.VMEM)
    return pl.pallas_call(
        functools.partial(output_kernel, count, rows, start),
        in_specs=[pl.BlockSpec(memory_space=pltpu.SMEM)] + [in_vmem] * len(operands),
        out_specs=in_vmem,
        scratch_shapes=[pltpu.VMEM(shape, jnp.float32)],
        out_shape=jax.ShapeDtypeStruct(shape, jnp.bfloat16 if last else jnp.float32),
        compiler_params=pltpu.CompilerParams(vmem_limit_bytes=28 * MIB),
        cost_estimate=pl.CostEstimate(
            flops=2 * shape[0] * depth * columns,
            bytes_accessed=2 * depth * columns + 2 * shape[0] * (depth + columns),
            transcendentals=0,
        ),
    )(me, *operands)


def rotation():
    half_dim = HEAD_SIZE // 2
    frequency = jnp.float32(500000.0) ** (
        -jnp.arange(half_dim, dtype=jnp.float32) * 2.0 / HEAD_SIZE
    )
    angles = jnp.float32(CONTEXT_LENGTH) * frequency
    return jnp.cos(angles), jnp.sin(angles)


def apply_rotary(tensor):
    half_dim = HEAD_SIZE // 2
    cosine, sine_part = rotation()
    first_half = tensor[..., :half_dim]
    second_half = tensor[..., half_dim:]
    return jnp.concatenate(
        [
            first_half * cosine - second_half * sine_part,
            second_half * cosine + first_half * sine_part,
        ],
        axis=-1,
    )


def attend(query_rows, fresh_keys, fresh_values, cache_keys, value_cache_rows):
    count_of_rows, heads = fresh_keys.shape[:2]
    grouped_queries = query_rows.reshape(count_of_rows, heads, GROUP, HEAD_SIZE)
    scaling = 1.0 / jnp.sqrt(jnp.float32(HEAD_SIZE))
    cached_scores = (
        jnp.einsum(
            "rkgd,rtkd->rkgt", grouped_queries, cache_keys, preferred_element_type=jnp.float32
        )
        * scaling
    )
    own_scores = (
        jnp.sum(
            grouped_queries.astype(jnp.float32) * fresh_keys.astype(jnp.float32)[:, :, None, :],
            axis=-1,
        )
        * scaling
    )
    highest = jnp.maximum(jnp.max(cached_scores, axis=-1), own_scores)
    cached_exp = jnp.exp(cached_scores - highest[..., None])
    own_exp = jnp.exp(own_scores - highest)
    denominator = jnp.sum(cached_exp, axis=-1) + own_exp
    cached_weights = (cached_exp / denominator[..., None]).astype(jnp.bfloat16)
    own_weights = (own_exp / denominator).astype(jnp.bfloat16)
    combined = jnp.einsum(
        "rkgt,rtkd->rkgd", cached_weights, value_cache_rows, preferred_element_type=jnp.float32
    )
    combined = (
        combined
        + own_weights.astype(jnp.float32)[..., None]
        * fresh_values.astype(jnp.float32)[:, :, None, :]
    )
    return combined.reshape(count_of_rows, heads * GROUP * HEAD_SIZE).astype(jnp.bfloat16)


def swap(value, count, phase=None, stage=None):
    orders = None if phase is None else stage_bits(count, phase)
    partners = []
    for i in range(count):
        mask = 1 if phase is None else orders[parity(i, count)][stage] ^ 1
        partners.append((i, i ^ mask))
    return lax.ppermute(value, "gx", partners)


def tie(value, token):
    return lax.optimization_barrier((value, token))[0]


class Reduction:
    def __init__(self, send, keep, count, rows, chunk):
        self.chunk = chunk
        self.keep, self.count, self.rows = keep, count, rows
        self.size = count // 2
        self.received = [swap(send, count)]

    def combine(self, part):
        total = self.keep[part]
        for piece in self.received:
            total = total + piece[part].astype(jnp.float32)
        return total

    def stage(self):
        self.size //= 2
        part = slice(self.size * self.rows, 2 * self.size * self.rows)
        send = self.combine(part).astype(jnp.bfloat16)
        self.received.append(swap(send, self.count, self.chunk, len(self.received) - 1))
        return send

    def own(self):
        return self.combine(slice(0, self.rows))


def body(count, activations, norm_gain, w_qkv, w_out, cache_keys, value_cache_rows):
    rows = cache_keys.shape[0]
    me = lax.axis_index("gx").astype(jnp.int32)[None]
    activations, norm_gain, w_qkv = [
        pltpu.with_memory_space_constraint(value, pltpu.HBM)
        for value in (activations, norm_gain, w_qkv)
    ]
    per_head = GROUP * HEAD_SIZE

    spans = []
    for order, (low, high) in enumerate(CHUNKS):
        start = low * per_head
        spans.append((start, (high * per_head if order else QKVW) - start))
    parts = []
    for send, keep in project(me, activations, norm_gain, w_qkv, count, rows, spans):
        parts.append(Reduction(send, keep, count, rows, len(parts)))
    w_out = tie(w_out, send)
    stages = len(stage_bits(count, 0)[0])
    for stage in range(stages):
        for part in parts:
            token = part.stage()
        if stage == 0:
            cache_keys = tie(cache_keys, token)
            value_cache_rows = tie(value_cache_rows, token)
    gathered = []
    for order, (low, high) in enumerate(CHUNKS):
        width = (high - low) * per_head
        if order > 0:
            parts[order].keep = tie(parts[order].keep, gathered[-1])
        sums = parts[order].own()
        if order == 0:
            own_squares = jnp.sum(sums[:, -LANES:], axis=1)
            inverse_rms = lax.rsqrt(own_squares / D + 1e-05)[:, None]
            fresh = sums[:, width:-LANES] * inverse_rms
            kv_width = KEY_VALUE_HEADS * HEAD_SIZE
            shape = (rows, KEY_VALUE_HEADS, HEAD_SIZE)
            fresh_keys = apply_rotary(fresh[:, :kv_width].reshape(shape)).astype(jnp.bfloat16)
            fresh_values = fresh[:, kv_width:].reshape(shape).astype(jnp.bfloat16)
        queries = apply_rotary(
            (sums[:, :width] * inverse_rms).reshape(rows, width // HEAD_SIZE, HEAD_SIZE)
        ).astype(jnp.bfloat16)
        gathered.append(
            attend(
                queries,
                fresh_keys[:, low:high],
                fresh_values[:, low:high],
                cache_keys[:, :, low:high],
                value_cache_rows[:, :, low:high],
            )
        )

    for stage in reversed(range(stages)):
        before = None
        for order in range(len(CHUNKS)):
            mine = gathered[order]
            if before is not None:
                mine = tie(mine, before)
            before = mine
            gathered[order] = jnp.concatenate([mine, swap(mine, count, GATHER, stage)], axis=0)
    total = None
    for order, (low, high) in enumerate(CHUNKS):
        mine = gathered[order]
        other = swap(mine, count)
        total = output_part(
            me, mine, other, w_out, total, count, rows, low * per_head,
            order == len(CHUNKS) - 1,
        )
    return total


def solution(mesh):
    return jax.shard_map(
        functools.partial(body, mesh.shape["gx"]),
        mesh=mesh,
        in_specs=(
            P("groups", "gx"),
            P("gx"),
            P("gx", None),
            P(None, "gx"),
            P(("groups", "gx"), None, None, None),
            P(("groups", "gx"), None, None, None),
        ),
        out_specs=P("groups", "gx"),
        check_vma=False,
    )
```
